32 devices in a mesh: ia: 2 (over y), ja: 4 (over z), ka: 4 (over x, core).
Axes of the slice: x: 2, y: 2, z: 4, core: 2. Of those that a mesh axis runs over, the one named last changes fastest.
Arguments:
- blocks: bfloat16 [32, 64, 64, 128], P(('ia', 'ja', 'ka')), may hold values from -6 to 6
- coords: int32 [3, 32], P(None, ('ia', 'ja', 'ka')), may hold values from 0 to 15, as said below
- live: int32 [32], P(('ia', 'ja', 'ka')), may hold values from 1 to 1, as said below
- factor_b: float32 [1024, 128], P('ja'), may hold values from -0.9 to 12
- factor_c: float32 [2048, 128], P('ka'), may hold values from -0.9 to 12
Outputs:
- loading_a: float32 [512, 128], P('ia')
- loading_b: float32 [1024, 128], P('ja')
- loading_c: float32 [2048, 128], P('ka')
The draws below stay inside these ranges and needn't reach their ends.
Inputs may be any that keep to these rules, and one draw needn't show every extreme that they name: `live`: slot d holds the block of device d (devices counted along ia, ja, ka, ia slowest). The slots of device (p, q, s) name blocks with coords[0] from p * 4 to p * 4 + 3, coords[1] from q * 4 to q * 4 + 3, coords[2] from s * 4 to s * 4 + 3; each device's slot names one block of its own 4 x 4 x 4 block region.
All inputs are finite; a program needn't handle non-finite values.
Results may differ from the reference program's by a relative error of at most 0.0057.
Values sent between devices are 32-bit elements; how exact they have to be, the bound alone decides.
A program may use at most 64 MiB of HBM per device.

```python
import jax
import jax.numpy as jnp
from jax import lax

RANK = 128
BI = 64
BJ = 64
BK = 128
GI_DEV = 4
GJ_DEV = 4
GK_DEV = 4
SLOTS = 1
ROWS_I = 512
ROWS_J = 1024
ROWS_K = 2048
ALL_SLOTS = 32
N_IA = 2
N_JA = 4
N_KA = 4


def draw_coords(key, part):
    devices_all = N_IA * N_JA * N_KA
    cell_count = GI_DEV * GJ_DEV * GK_DEV
    key_list = jax.random.split(key, devices_all)
    chosen = jax.vmap(lambda single: jax.random.permutation(single, cell_count)[:SLOTS])(key_list)
    device = jnp.arange(devices_all, dtype=jnp.int32)[:, None]
    plane_i = device // (N_JA * N_KA)
    plane_j = device // N_KA % N_JA
    plane_k = device % N_KA
    local_i = chosen // (GJ_DEV * GK_DEV)
    local_j = chosen // GK_DEV % GJ_DEV
    local_k = chosen % GK_DEV
    stacked = jnp.stack([(plane_i * GI_DEV + local_i).reshape(-1), (plane_j * GJ_DEV + local_j).reshape(-1), (plane_k * GK_DEV + local_k).reshape(-1)])
    return stacked.astype(jnp.int32)


def draw_live(key, part):
    devices_all = N_IA * N_JA * N_KA
    drawn = jax.random.randint(key, (devices_all,), 0, SLOTS)
    counts = 1 + drawn * drawn // max(SLOTS - 1, 1)
    busiest = jax.random.randint(jax.random.fold_in(key, 11), (), 0, devices_all)
    return counts.at[busiest].set(SLOTS).astype(jnp.int32)


def factor_rows(key, count_rows):
    return 0.6 + 0.3 * jax.random.truncated_normal(key, -3.0, 3.0, (count_rows, RANK), jnp.float32)


def draw_factor_b(key, part):
    return factor_rows(key, ROWS_J)


def draw_factor_c(key, part):
    return factor_rows(key, ROWS_K)


def shard_levels(key, shape, cuts, least, top_value):
    def one(position, shards_of):
        draws = jax.random.uniform(jax.random.fold_in(jax.random.fold_in(key, 6), position), (shards_of,), jnp.float32, least / len(cuts), top_value / len(cuts))
        return jnp.repeat(jnp.exp(draws), shape[position] // shards_of).reshape((-1,) + (1,) * (len(shape) - position - 1))

    loudness = one(*cuts[0])
    for cut in cuts[1:]:
        loudness = loudness * one(*cut)
    return loudness


def centred(key, shape, spread, limit, pieces=(), kind=jnp.bfloat16):
    array = spread * jax.random.normal(key, shape, jnp.float32)
    if pieces:
        array = array * shard_levels(key, shape, pieces, -0.22, 0.18)
    return jnp.clip(array, -limit, limit).astype(kind)


def setup_inputs(seed: int = 0) -> dict:
    streams_of = jax.random.split(jax.random.key(seed), 6)
    return {
        "blocks": centred(streams_of[0], (ALL_SLOTS, BI, BJ, BK), 1.0, 6.0, ((0, 32),)),
        "coords": draw_coords(jax.random.fold_in(streams_of[5], 71), 0),
        "live": draw_live(jax.random.fold_in(streams_of[5], 71), 0),
        "factor_b": draw_factor_b(jax.random.fold_in(streams_of[5], 71), 0),
        "factor_c": draw_factor_c(jax.random.fold_in(streams_of[5], 71), 0),
    }


RIDGE_SHARE = 0.3
EPSILON = 1e-06
HIGHEST = lax.Precision.HIGHEST
sweep_order = (0, 1, 2)

def mean_gram(factor):
    return jnp.dot(factor.T.astype(jnp.float32), factor.astype(jnp.float32), precision=HIGHEST, preferred_element_type=jnp.float32) / factor.shape[0]

def factorize(gram_one, gram_two):
    merged = gram_one * gram_two
    order_rank = merged.shape[0]
    shift_value = RIDGE_SHARE * jnp.trace(merged) / order_rank
    lower_factor = jnp.linalg.cholesky(merged + shift_value * jnp.eye(order_rank, dtype=jnp.float32))
    return lax.linalg.triangular_solve(lower_factor, jnp.eye(order_rank, dtype=jnp.float32), left_side=True, lower=True)

def apply_inverse(inverse_lower, values):
    middle = jnp.dot(values.astype(jnp.float32), inverse_lower.T.astype(jnp.float32), precision=HIGHEST, preferred_element_type=jnp.float32)
    return jnp.dot(middle.astype(jnp.float32), inverse_lower.astype(jnp.float32), precision=HIGHEST, preferred_element_type=jnp.float32)

def normalize(solved):
    squares = lax.optimization_barrier(jnp.sum(solved * solved, axis=0)) / solved.shape[0]
    scaled = solved * lax.rsqrt(squares + EPSILON)
    return (scaled, mean_gram(scaled))

def block_product(mode_now, tensor_block, rows_one, rows_two):
    khatri = (rows_one[:, None, :] * rows_two[None, :, :]).astype(jnp.bfloat16)
    kept_dims = tuple((axis_id for axis_id in range(3) if axis_id != mode_now))
    return lax.dot_general(tensor_block.astype(jnp.float32), khatri.astype(jnp.float32), ((kept_dims, (0, 1)), ((), ())), precision=HIGHEST, preferred_element_type=jnp.float32)

def mttkrp(mode_now, blocks, coords, live, factors, length_rows):
    extents = (BI, BJ, BK)
    others = tuple((axis_id for axis_id in range(3) if axis_id != mode_now))
    slot_ids = jnp.arange(blocks.shape[0], dtype=jnp.int32)
    active = slot_ids % SLOTS < jnp.repeat(live, SLOTS)

    def visit(summed, slot_index):

        def accumulate(carried):
            tensor_block = lax.dynamic_index_in_dim(blocks, slot_index, 0, keepdims=False)
            rows_one = lax.dynamic_slice_in_dim(factors[others[0]], (coords[others[0], slot_index] * extents[others[0]]).astype(jnp.int32), extents[others[0]], 0)
            rows_two = lax.dynamic_slice_in_dim(factors[others[1]], (coords[others[1], slot_index] * extents[others[1]]).astype(jnp.int32), extents[others[1]], 0)
            product_rows = block_product(mode_now, tensor_block, rows_one, rows_two)
            offset = (coords[mode_now, slot_index] * extents[mode_now]).astype(jnp.int32)
            current = lax.dynamic_slice_in_dim(carried, offset, extents[mode_now], 0)
            return lax.dynamic_update_slice_in_dim(carried, current + product_rows, offset, 0)

        def unchanged(carried):
            return carried
        return (lax.cond(active[slot_index], accumulate, unchanged, summed), None)
    start_rows = jnp.zeros((length_rows, RANK), jnp.float32)
    return lax.scan(visit, start_rows, slot_ids)[0]

def reference(blocks, coords, live, factor_b, factor_c):
    lengths = (ROWS_I, ROWS_J, ROWS_K)
    factors = [jnp.zeros((ROWS_I, RANK), jnp.float32), factor_b, factor_c]
    gram_list = [None, mean_gram(factor_b), mean_gram(factor_c)]
    for mode_now in sweep_order:
        others = tuple((axis_id for axis_id in range(3) if axis_id != mode_now))
        summed = mttkrp(mode_now, blocks, coords, live, factors, lengths[mode_now])
        inverse_lower = factorize(gram_list[others[0]], gram_list[others[1]])
        factors[mode_now], gram_list[mode_now] = normalize(apply_inverse(inverse_lower, summed))
    return (factors[0], factors[1], factors[2])
```

```python
import functools

import jax
import jax.numpy as jnp
from jax import lax
from jax.experimental import pallas as pl
from jax.experimental.pallas import tpu as pltpu
from jax.sharding import PartitionSpec as P

GI_DEV = 4
RIDGE_SHARE = 0.3
EPSILON = 1e-06
HIGHEST = lax.Precision.HIGHEST
MESH = pl.DeviceIdType.MESH
F32 = jnp.float32
BF16 = jnp.bfloat16
CHUNK = 8


def newton_plan(order):
    low = RIDGE_SHARE / order
    high = 1.0 + low
    first = 2.0 / (low + high)
    error = (high - low) / (high + low)
    scales = []
    while error > 1e-9:
        square = error * error
        scales.append(2.0 / (2.0 - square))
        error = square / (2.0 - square)
    return first, scales


def dot_high(left, right):
    return jnp.dot(left, right, precision=HIGHEST, preferred_element_type=F32)


def system_inverse(gram_one, gram_two):
    order = gram_one.shape[0]
    merged = gram_one * gram_two
    on_diagonal = lax.broadcasted_iota(jnp.int32, (order, order), 0) == lax.broadcasted_iota(
        jnp.int32, (order, order), 1
    )
    eye = jnp.where(on_diagonal, 1.0, 0.0).astype(F32)
    trace = jnp.sum(jnp.sum(merged * eye, axis=1, keepdims=True), axis=0, keepdims=True)
    unit = 1.0 / trace
    system = merged * unit + (RIDGE_SHARE / order) * eye
    first, scales = newton_plan(order)
    twice = 2.0 * eye
    guess = (scales[0] * first) * (twice - first * system)
    for scale in scales[1:]:
        residual = twice - dot_high(system, guess)
        guess = scale * dot_high(guess, residual)
    return guess * unit


def gram_of(values):
    return lax.dot_general(
        values, values, (((0,), (0,)), ((), ())), precision=HIGHEST, preferred_element_type=F32
    )


def kernel(
    sizes,
    coords,
    tensor,
    factor_b,
    factor_c,
    out_a,
    out_b,
    out_c,
    wide,
    turned,
    rows_one,
    gram_b_buf,
    gram_c_buf,
    send_0,
    send_1,
    send_2,
    take_0,
    take_1,
    take_2,
    share_0,
    share_1,
    share_2,
    sums,
    gram_b_sems,
    gram_c_sems,
    cut_sems_0,
    cut_sems_1,
    cut_sems_2,
    spread_sems_0,
    spread_sems_1,
    spread_sems_2,
    sum_sems,
):
    n_i, n_j, n_k = sizes
    n_all = n_i * n_j * n_k
    p, q, s = lax.axis_index("ia"), lax.axis_index("ja"), lax.axis_index("ka")
    me = (p * n_j + q) * n_k + s
    spans = (out_a.shape[0], out_b.shape[0], out_c.shape[0])
    extents = (turned.shape[1], turned.shape[0], turned.shape[2])
    counts = tuple(span // extent for span, extent in zip(spans, extents))

    def everyone(index):
        return (index // (n_j * n_k), (index // n_k) % n_j, index % n_k)

    groups = (
        (n_j * n_k, q * n_k + s, lambda u: (p, u // n_k, u % n_k)),
        (n_i * n_k, p * n_k + s, lambda u: (u // n_k, q, u % n_k)),
        (n_i * n_j, p * n_j + q, lambda u: (u // n_j, u % n_j, s)),
    )
    all_group = (n_all, me, everyone)
    ja_group = (n_j, q, lambda u: (p, u, s))
    ka_group = (n_k, s, lambda u: (p, q, u))

    def partners(group, body):
        size, mine, place = group

        @pl.loop(1, size)
        def _(offset):
            other = lax.rem(mine + offset, size)
            body(other, place(other))

    def copy(source, target, sems, mine, other, device):
        return pltpu.make_async_remote_copy(
            src_ref=source,
            dst_ref=target,
            send_sem=sems.at[0, other],
            recv_sem=sems.at[1, mine],
            device_id=device,
            device_id_type=MESH,
        )

    def spread(group, buffer, sems):
        mine = group[1]

        def body(other, device):
            copy(buffer.at[mine], buffer.at[mine], sems, mine, other, device).start()

        partners(group, body)

    def arrive(group, buffer, sems):
        def body(other, device):
            copy(buffer.at[other], buffer.at[other], sems, other, other, device).wait_recv()

        partners(group, body)

    def sent(group, buffer, sems):
        mine = group[1]

        def body(other, device):
            copy(buffer.at[mine], buffer.at[mine], sems, mine, other, device).wait_send()

        partners(group, body)

    barrier = pltpu.get_barrier_semaphore()

    def greet(other, device):
        pl.semaphore_signal(barrier, inc=1, device_id=device, device_id_type=MESH)

    partners(all_group, greet)
    gram_b_buf[q] = gram_of(factor_b[...])
    gram_c_buf[s] = gram_of(factor_c[...])
    pl.semaphore_wait(barrier, n_all - 1)
    spread(ja_group, gram_b_buf, gram_b_sems)
    spread(ka_group, gram_c_buf, gram_c_sems)

    def marks_of(mode, base):
        row = lax.broadcasted_iota(jnp.int32, (counts[mode], out_a.shape[1]), 0) + base
        return jnp.where(row == jnp.full(row.shape, coords[mode, 0], jnp.int32), 1.0, 0.0)

    marks = (marks_of(0, p * counts[0]), marks_of(1, q * counts[1]), marks_of(2, s * counts[2]))

    def block_rows(mode, source):
        extent = extents[mode]
        return sum(
            source[g * extent : (g + 1) * extent, :] * marks[mode][g : g + 1, :]
            for g in range(counts[mode])
        )

    wide[...] = tensor[...].astype(F32)

    @pl.loop(0, extents[1])
    def _(b):
        turned[b] = wide[pl.ds(b, extents[0], stride=extents[1]), :].astype(BF16)

    def product(mode, rows_of_one, rows_of_two):
        rows_one[0 : rows_of_one.shape[0], :] = rows_of_one
        total = jnp.zeros((extents[mode], rows_of_two.shape[1]), F32)

        def step(j, total):
            ones = rows_one[pl.ds(pl.multiple_of(j * CHUNK, CHUNK), CHUNK), :]
            khatri = jnp.concatenate(
                [(ones[i : i + 1, :] * rows_of_two).astype(BF16) for i in range(CHUNK)], axis=0
            )
            if mode == 2:
                depth = CHUNK * extents[1]
                left = tensor[pl.ds(pl.multiple_of(j * depth, depth), depth), :]
                dims = (((0,), (0,)), ((), ()))
            else:
                if mode == 0:
                    parts = [turned[j * CHUNK + i] for i in range(CHUNK)]
                else:
                    parts = [
                        tensor[pl.ds(pl.multiple_of((j * CHUNK + i) * extents[1], extents[1]), extents[1]), :]
                        for i in range(CHUNK)
                    ]
                left = jnp.concatenate(parts, axis=1)
                dims = (((1,), (0,)), ((), ()))
            return total + lax.dot_general(left, khatri, dims, preferred_element_type=F32)

        return lax.fori_loop(0, rows_of_one.shape[0] // CHUNK, step, total)

    def cut(mode, rows, send, take, sems):
        size, mine, _ = groups[mode]
        share = extents[mode] // size
        for u in range(size):
            send[u, 0:share, :] = rows[u * share : (u + 1) * share, :]
            send[u, share : share + counts[mode], :] = marks[mode]

        def body(other, device):
            copy(send.at[other], take.at[mine], sems, mine, other, device).start()

        partners(groups[mode], body)

    def gather_cut(mode, send, take, sems):
        size, mine, _ = groups[mode]
        share, count = extents[mode] // size, counts[mode]

        def add(total, buffer, index):
            rows = buffer[index, 0:share, :]
            return tuple(
                total[g] + rows * buffer[index, share + g : share + g + 1, :] for g in range(count)
            )

        total = tuple(jnp.zeros((share, out_a.shape[1]), F32) for _ in range(count))
        total = add(total, send, mine)

        def body(offset, total):
            other = lax.rem(mine + offset, size)
            place = groups[mode][2](other)
            copy(send.at[other], take.at[other], sems, other, other, place).wait_recv()
            return add(total, take, other)

        total = lax.fori_loop(1, size, body, total)
        return jnp.concatenate(total, axis=0)

    def cut_sent(mode, send, take, sems):
        mine = groups[mode][1]

        def body(other, device):
            copy(send.at[other], take.at[mine], sems, mine, other, device).wait_send()

        partners(groups[mode], body)

    def place_rows(mode, out, buffer, slot_of, scale):
        size = groups[mode][0]
        share = extents[mode] // size
        for u in range(size):
            rows = buffer[slot_of(u)] * scale
            for g in range(counts[mode]):
                start = g * extents[mode] + u * share
                out[start : start + share, :] = rows[g * share : (g + 1) * share, :]

    lengths = (spans[0] * n_i, spans[1] * n_j, spans[2] * n_k)

    def finish(mode, shares, out, slot_of):
        rows = shares[...].reshape(lengths[mode], out.shape[1])
        squares = jnp.sum(rows * rows, axis=0, keepdims=True) / lengths[mode]
        scale = lax.rsqrt(squares + EPSILON)
        place_rows(mode, out, shares, slot_of, scale)
        return gram_of(rows * scale) / lengths[mode]

    rows = product(0, block_rows(1, factor_b), block_rows(2, factor_c))
    cut(0, rows, send_0, take_0, cut_sems_0)
    arrive(ja_group, gram_b_buf, gram_b_sems)
    arrive(ka_group, gram_c_buf, gram_c_sems)
    gram_b = jnp.sum(gram_b_buf[...], axis=0) / lengths[1]
    gram_c = jnp.sum(gram_c_buf[...], axis=0) / lengths[2]
    inverse = system_inverse(gram_b, gram_c)
    share_0[me] = dot_high(gather_cut(0, send_0, take_0, cut_sems_0), inverse)
    spread(all_group, share_0, spread_sems_0)
    arrive(all_group, share_0, spread_sems_0)
    gram_a = finish(0, share_0, out_a, lambda u: p * groups[0][0] + u)

    rows = product(1, block_rows(0, out_a), block_rows(2, factor_c))
    cut(1, rows, send_1, take_1, cut_sems_1)
    inverse = system_inverse(gram_a, gram_c)
    share_1[me] = dot_high(gather_cut(1, send_1, take_1, cut_sems_1), inverse)
    spread(all_group, share_1, spread_sems_1)
    arrive(all_group, share_1, spread_sems_1)
    gram_b = finish(1, share_1, out_b, lambda u: ((u // n_k) * n_j + q) * n_k + u % n_k)

    rows = product(2, block_rows(0, out_a), block_rows(1, out_b))
    cut(2, rows, send_2, take_2, cut_sems_2)
    inverse = system_inverse(gram_a, gram_b)
    solved = dot_high(gather_cut(2, send_2, take_2, cut_sems_2), inverse)
    mine = groups[2][1]
    share_2[mine] = solved
    sums[me] = jnp.broadcast_to(jnp.sum(solved * solved, axis=0, keepdims=True), sums.shape[1:])
    spread(all_group, sums, sum_sems)
    spread(groups[2], share_2, spread_sems_2)
    arrive(all_group, sums, sum_sems)
    arrive(groups[2], share_2, spread_sems_2)
    squares = jnp.sum(sums[...], axis=0)[0:1, :] / lengths[2]
    place_rows(2, out_c, share_2, lambda u: u, lax.rsqrt(squares + EPSILON))

    sent(ja_group, gram_b_buf, gram_b_sems)
    sent(ka_group, gram_c_buf, gram_c_sems)
    cut_sent(0, send_0, take_0, cut_sems_0)
    cut_sent(1, send_1, take_1, cut_sems_1)
    cut_sent(2, send_2, take_2, cut_sems_2)
    sent(all_group, share_0, spread_sems_0)
    sent(all_group, share_1, spread_sems_1)
    sent(groups[2], share_2, spread_sems_2)
    sent(all_group, sums, sum_sems)


def on_device(sizes, blocks, coords, live, factor_b, factor_c):
    n_i, n_j, n_k = sizes
    n_all = n_i * n_j * n_k
    slots, bi, bj, bk = blocks.shape
    rank = factor_b.shape[1]
    span_a, span_b, span_c = GI_DEV * bi, factor_b.shape[0], factor_c.shape[0]
    group_sizes = (n_j * n_k, n_i * n_k, n_i * n_j)
    spans = (span_a, span_b, span_c)
    extents = (bi, bj, bk)

    def message(mode):
        rows = extents[mode] // group_sizes[mode] + spans[mode] // extents[mode]
        return (group_sizes[mode], (rows + 7) // 8 * 8, rank)

    def buffer(*shape):
        return pltpu.VMEM(shape, F32)

    vmem = pl.BlockSpec(memory_space=pltpu.VMEM)
    return pl.pallas_call(
        functools.partial(kernel, sizes),
        out_shape=[jax.ShapeDtypeStruct((span, rank), F32) for span in spans],
        in_specs=[pl.BlockSpec(memory_space=pltpu.SMEM), vmem, vmem, vmem],
        out_specs=[vmem] * 3,
        scratch_shapes=[
            buffer(bi * bj, bk),
            pltpu.VMEM((bj, bi, bk), BF16),
            buffer(max(bi, bj), rank),
            buffer(n_j, rank, rank),
            buffer(n_k, rank, rank),
            *[buffer(*message(mode)) for mode in range(3)],
            *[buffer(*message(mode)) for mode in range(3)],
            buffer(n_all, span_a // group_sizes[0], rank),
            buffer(n_all, span_b // group_sizes[1], rank),
            buffer(group_sizes[2], span_c // group_sizes[2], rank),
            buffer(n_all, 8, rank),
            pltpu.SemaphoreType.DMA((2, n_j)),
            pltpu.SemaphoreType.DMA((2, n_k)),
            *[pltpu.SemaphoreType.DMA((2, size)) for size in group_sizes],
            pltpu.SemaphoreType.DMA((2, n_all)),
            pltpu.SemaphoreType.DMA((2, n_all)),
            pltpu.SemaphoreType.DMA((2, group_sizes[2])),
            pltpu.SemaphoreType.DMA((2, n_all)),
        ],
        compiler_params=pltpu.CompilerParams(
            collective_id=0, has_side_effects=True, vmem_limit_bytes=40 * 1024 * 1024
        ),
    )(coords, blocks.reshape(slots * bi * bj, bk), factor_b, factor_c)


def solution(mesh):
    sizes = (mesh.shape["ia"], mesh.shape["ja"], mesh.shape["ka"])
    placed = (
        P(("ia", "ja", "ka"), None, None, None),
        P(None, ("ia", "ja", "ka")),
        P(("ia", "ja", "ka")),
        P("ja", None),
        P("ka", None),
    )
    return jax.shard_map(
        functools.partial(on_device, sizes),
        mesh=mesh,
        in_specs=placed,
        out_specs=(P("ia", None), P("ja", None), P("ka", None)),
        check_vma=False,
    )
```

```python
import functools

import jax
import jax.numpy as jnp
from jax import lax
from jax.experimental import pallas as pl
from jax.experimental.pallas import tpu as pltpu
from jax.sharding import PartitionSpec as P

GI_DEV = 4
RIDGE_SHARE = 0.3
EPSILON = 1e-06
HIGHEST = lax.Precision.HIGHEST
MESH = pl.DeviceIdType.MESH
F32 = jnp.float32
BF16 = jnp.bfloat16
CHUNK = 8


def newton_plan(order):
    low = RIDGE_SHARE / order
    high = 1.0 + low
    first = 2.0 / (low + high)
    error = (high - low) / (high + low)
    scales = []
    while error > 1e-9:
        square = error * error
        scales.append(2.0 / (2.0 - square))
        error = square / (2.0 - square)
    return first, scales


def dot_high(left, right):
    return jnp.dot(left, right, precision=HIGHEST, preferred_element_type=F32)


def halves(values):
    head = values.astype(BF16)
    return head, (values - head.astype(F32)).astype(BF16)


def dot_middle(left, right):
    left_head, left_tail = halves(left)
    right_head, right_tail = halves(right)

    def times(one, two):
        return jnp.dot(one, two, preferred_element_type=F32)

    return times(left_head, right_head) + (
        times(left_head, right_tail) + times(left_tail, right_head)
    )


def system_inverse(gram_one, gram_two):
    order = gram_one.shape[0]
    merged = gram_one * gram_two
    on_diagonal = lax.broadcasted_iota(jnp.int32, (order, order), 0) == lax.broadcasted_iota(
        jnp.int32, (order, order), 1
    )
    eye = jnp.where(on_diagonal, 1.0, 0.0).astype(F32)
    trace = jnp.sum(jnp.sum(merged * eye, axis=1, keepdims=True), axis=0, keepdims=True)
    unit = 1.0 / trace
    system = merged * unit + (RIDGE_SHARE / order) * eye
    first, scales = newton_plan(order)
    twice = 2.0 * eye
    guess = (scales[0] * first) * (twice - first * system)
    for step, scale in enumerate(scales[1:], 1):
        times = dot_high if step + 2 >= len(scales) else dot_middle
        residual = twice - times(system, guess)
        guess = scale * times(guess, residual)
    return guess * unit


def gram_of(values):
    return lax.dot_general(
        values, values, (((0,), (0,)), ((), ())), precision=HIGHEST, preferred_element_type=F32
    )


def kernel(
    sizes,
    coords,
    tensor_hbm,
    factor_b_hbm,
    factor_c_hbm,
    out_a,
    out_b,
    out_c,
    tensor,
    factor_b,
    factor_c,
    wide,
    turned,
    rows_one,
    plane_b,
    slices_b,
    whole_b,
    gram_c_buf,
    plane_a_buf,
    plane_2,
    slices_2,
    whole_2,
    send_0,
    send_1,
    send_2,
    take_0,
    take_1,
    take_2,
    share_0,
    share_1,
    share_2,
    sums_0,
    sums_1,
    sums_2,
    load_sems,
    sems,
):
    n_i, n_j, n_k = sizes
    n_all = n_i * n_j * n_k
    p, q, s = lax.axis_index("ia"), lax.axis_index("ja"), lax.axis_index("ka")
    spans = (out_a.shape[0], out_b.shape[0], out_c.shape[0])
    extents = (turned.shape[1], turned.shape[0], turned.shape[2])
    counts = tuple(span // extent for span, extent in zip(spans, extents))
    lengths = (spans[0] * n_i, spans[1] * n_j, spans[2] * n_k)
    rank = out_a.shape[1]

    loads = [
        pltpu.make_async_copy(source, target, load_sems.at[i])
        for i, (source, target) in enumerate(
            ((factor_b_hbm, factor_b), (factor_c_hbm, factor_c), (tensor_hbm, tensor))
        )
    ]
    for load in loads:
        load.start()

    position = (p, q, s)
    shifted = [
        [lax.rem(place + offset, size) for offset in range(size)]
        for place, size in zip(position, sizes)
    ]

    class Group:
        def __init__(self, *axes):
            self.axes = axes
            self.size = 1
            self.mine = 0
            for axis in axes:
                self.size *= sizes[axis]
                self.mine = self.mine * sizes[axis] + position[axis]

        def partners(self, body):
            if self.size <= 32:
                for offset in range(1, self.size):
                    device, other, rest = list(position), 0, []
                    for axis in reversed(self.axes):
                        rest.append(offset % sizes[axis])
                        offset //= sizes[axis]
                    for axis, step in zip(self.axes, reversed(rest)):
                        device[axis] = shifted[axis][step]
                        other = other * sizes[axis] + device[axis]
                    body(other, tuple(device))
            else:

                @pl.loop(1, self.size)
                def _(offset):
                    other = lax.rem(self.mine + offset, self.size)
                    device, rest = list(position), other
                    for axis in reversed(self.axes):
                        device[axis] = lax.rem(rest, sizes[axis])
                        rest = rest // sizes[axis]
                    body(other, tuple(device))

    everyone = Group(0, 1, 2)
    groups = (Group(1, 2), Group(0, 2), Group(0, 1))
    lines = (Group(0), Group(1), Group(2))
    me = everyone.mine

    def copy(source, target, phase, device):
        return pltpu.make_async_remote_copy(
            src_ref=source,
            dst_ref=target,
            send_sem=sems.at[0, phase],
            recv_sem=sems.at[1, phase],
            device_id=device,
            device_id_type=MESH,
        )

    def all_but_one(group, buffer, phase):
        part = buffer.at[pl.ds(0, group.size - 1)]
        return copy(part, part, phase, tuple(row[-1] for row in shifted))

    def spread(group, buffer, phase):
        slot = buffer.at[group.mine]
        group.partners(lambda other, device: copy(slot, slot, phase, device).start())

    def deal(group, source, target, phase):
        group.partners(
            lambda other, device: copy(
                source.at[other], target.at[group.mine], phase, device
            ).start()
        )

    def arrive(group, buffer, phase):
        all_but_one(group, buffer, phase).wait_recv()

    def sent(group, buffer, phase):
        all_but_one(group, buffer, phase).wait_send()

    barrier = pltpu.get_barrier_semaphore()
    everyone.partners(
        lambda other, device: pl.semaphore_signal(
            barrier, inc=1, device_id=device, device_id_type=MESH
        )
    )

    def store_slices(gram, plane):
        share = plane.shape[1]
        for u in range(plane.shape[0]):
            plane[u] = gram[u * share : (u + 1) * share, :]

    def start_slices(gram, plane, slices, phase):
        store_slices(gram, plane)
        mine = plane.at[groups[1].mine]
        target = slices.at[q]
        lines[1].partners(lambda other, device: copy(mine, target, phase, device).start())

    def turn_slices(plane, slices, whole, phase):
        arrive(lines[1], slices, phase)
        slices[q] = plane[groups[1].mine]
        whole[groups[1].mine] = jnp.sum(slices[...], axis=0)
        spread(groups[1], whole, phase + 1)

    def end_slices(whole, phase):
        arrive(groups[1], whole, phase + 1)
        return whole[...].reshape(rank, rank) / lengths[1]

    loads[0].wait()
    first_gram_b = gram_of(factor_b[...])
    loads[1].wait()
    gram_c_buf[s] = gram_of(factor_c[...])
    pl.semaphore_wait(barrier, n_all - 1)
    start_slices(first_gram_b, plane_b, slices_b, 0)
    spread(lines[2], gram_c_buf, 2)

    def marks_of(mode, base):
        row = lax.broadcasted_iota(jnp.int32, (counts[mode], rank), 0) + base
        return jnp.where(row == jnp.full(row.shape, coords[mode], jnp.int32), 1.0, 0.0)

    marks = (marks_of(0, p * counts[0]), marks_of(1, q * counts[1]), marks_of(2, s * counts[2]))

    def block_rows(mode, source):
        extent = extents[mode]
        return sum(
            source[g * extent : (g + 1) * extent, :] * marks[mode][g : g + 1, :]
            for g in range(counts[mode])
        )

    loads[2].wait()
    wide[...] = tensor[...].astype(F32)

    @pl.loop(0, extents[1], unroll=8)
    def _(b):
        turned[b] = wide[pl.ds(b, extents[0], stride=extents[1]), :].astype(BF16)

    def product(mode, rows_of_one, rows_of_two):
        rows_one[0 : rows_of_one.shape[0], :] = rows_of_one
        total = jnp.zeros((extents[mode], rank), F32)

        def step(j, total):
            ones = rows_one[pl.ds(pl.multiple_of(j * CHUNK, CHUNK), CHUNK), :]
            khatri = jnp.concatenate(
                [(ones[i : i + 1, :] * rows_of_two).astype(BF16) for i in range(CHUNK)], axis=0
            )
            if mode == 2:
                depth = CHUNK * extents[1]
                left = tensor[pl.ds(pl.multiple_of(j * depth, depth), depth), :]
                dims = (((0,), (0,)), ((), ()))
            else:
                if mode == 0:
                    parts = [turned[j * CHUNK + i] for i in range(CHUNK)]
                else:
                    height = extents[1]
                    parts = [
                        tensor[pl.ds(pl.multiple_of((j * CHUNK + i) * height, height), height), :]
                        for i in range(CHUNK)
                    ]
                left = jnp.concatenate(parts, axis=1)
                dims = (((1,), (0,)), ((), ()))
            return total + lax.dot_general(left, khatri, dims, preferred_element_type=F32)

        return lax.fori_loop(0, rows_of_one.shape[0] // CHUNK, step, total)

    def cut(mode, rows, send, take, phase):
        group = groups[mode]
        share = extents[mode] // group.size
        for u in range(group.size):
            send[u, 0:share, :] = rows[u * share : (u + 1) * share, :]
            send[u, share : share + counts[mode], :] = marks[mode]
        deal(group, send, take, phase)

    def gather_cut(mode, send, take, phase):
        group = groups[mode]
        share, count = extents[mode] // group.size, counts[mode]
        arrive(group, take, phase)
        take[group.mine] = send[group.mine]
        total = [jnp.zeros((share, rank), F32) for _ in range(count)]
        for u in range(group.size):
            rows = take[u, 0:share, :]
            for g in range(count):
                total[g] = total[g] + rows * take[u, share + g : share + g + 1, :]
        return jnp.concatenate(total, axis=0)

    def settle(mode, send, take, inverse, shares, sums, out, phase):
        group = groups[mode]
        share = extents[mode] // group.size
        solved = dot_high(gather_cut(mode, send, take, phase), inverse)
        shares[group.mine] = solved
        sums[me] = jnp.sum(solved * solved, axis=0, keepdims=True)
        spread(everyone, sums, phase + 1)
        spread(group, shares, phase + 2)
        arrive(everyone, sums, phase + 1)
        squares = jnp.sum(sums[...], axis=0) / lengths[mode]
        scale = lax.rsqrt(squares + EPSILON)
        arrive(group, shares, phase + 2)
        for u in range(group.size):
            rows = shares[u] * scale
            for g in range(counts[mode]):
                start = g * extents[mode] + u * share
                out[start : start + share, :] = rows[g * share : (g + 1) * share, :]

    rows = product(0, block_rows(1, factor_b), block_rows(2, factor_c))
    cut(0, rows, send_0, take_0, 3)
    turn_slices(plane_b, slices_b, whole_b, 0)
    arrive(lines[2], gram_c_buf, 2)
    gram_c = jnp.sum(gram_c_buf[...], axis=0) / lengths[2]
    gram_b = end_slices(whole_b, 0)
    inverse = system_inverse(gram_b, gram_c)
    settle(0, send_0, take_0, inverse, share_0, sums_0, out_a, 3)
    plane_a_buf[p] = gram_of(out_a[...])
    spread(lines[0], plane_a_buf, 6)

    rows = product(1, block_rows(0, out_a), block_rows(2, factor_c))
    cut(1, rows, send_1, take_1, 7)
    arrive(lines[0], plane_a_buf, 6)
    gram_a = jnp.sum(plane_a_buf[...], axis=0) / lengths[0]
    inverse = system_inverse(gram_a, gram_c)
    settle(1, send_1, take_1, inverse, share_1, sums_1, out_b, 7)
    start_slices(gram_of(out_b[...]), plane_2, slices_2, 10)

    rows = product(2, block_rows(0, out_a), block_rows(1, out_b))
    turn_slices(plane_2, slices_2, whole_2, 10)
    cut(2, rows, send_2, take_2, 12)
    gram_b = end_slices(whole_2, 10)
    inverse = system_inverse(gram_a, gram_b)
    settle(2, send_2, take_2, inverse, share_2, sums_2, out_c, 12)

    sent(lines[1], slices_b, 0)
    sent(groups[1], whole_b, 1)
    sent(lines[2], gram_c_buf, 2)
    sent(groups[0], send_0, 3)
    sent(everyone, sums_0, 4)
    sent(groups[0], share_0, 5)
    sent(lines[0], plane_a_buf, 6)
    sent(groups[1], send_1, 7)
    sent(everyone, sums_1, 8)
    sent(groups[1], share_1, 9)
    sent(lines[1], slices_2, 10)
    sent(groups[1], whole_2, 11)
    sent(groups[2], send_2, 12)
    sent(everyone, sums_2, 13)
    sent(groups[2], share_2, 14)


def on_device(sizes, blocks, coords, live, factor_b, factor_c):
    n_i, n_j, n_k = sizes
    n_all = n_i * n_j * n_k
    slots, bi, bj, bk = blocks.shape
    rank = factor_b.shape[1]
    group_sizes = (n_j * n_k, n_i * n_k, n_i * n_j)
    spans = (GI_DEV * bi, factor_b.shape[0], factor_c.shape[0])
    extents = (bi, bj, bk)

    def message(mode):
        rows = extents[mode] // group_sizes[mode] + spans[mode] // extents[mode]
        return (group_sizes[mode], (rows + 7) // 8 * 8, rank)

    def buffer(*shape):
        return pltpu.VMEM(shape, F32)

    slices = [
        buffer(group_sizes[1], rank // group_sizes[1], rank),
        buffer(n_j, rank // group_sizes[1], rank),
        buffer(group_sizes[1], rank // group_sizes[1], rank),
    ]
    vmem = pl.BlockSpec(memory_space=pltpu.VMEM)
    far = pl.BlockSpec(memory_space=pltpu.HBM)
    return pl.pallas_call(
        functools.partial(kernel, sizes),
        out_shape=[jax.ShapeDtypeStruct((span, rank), F32) for span in spans],
        in_specs=[pl.BlockSpec(memory_space=pltpu.SMEM), far, far, far],
        out_specs=[vmem] * 3,
        scratch_shapes=[
            pltpu.VMEM((bi * bj, bk), BF16),
            buffer(*factor_b.shape),
            buffer(*factor_c.shape),
            buffer(bi * bj, bk),
            pltpu.VMEM((bj, bi, bk), BF16),
            buffer(max(bi, bj), rank),
            *slices,
            buffer(n_k, rank, rank),
            buffer(n_i, rank, rank),
            *slices,
            *[buffer(*message(mode)) for mode in range(3)],
            *[buffer(*message(mode)) for mode in range(3)],
            *[buffer(group_sizes[mode], spans[mode] // group_sizes[mode], rank) for mode in range(3)],
            *[buffer(n_all, 1, rank) for mode in range(3)],
            pltpu.SemaphoreType.DMA((3,)),
            pltpu.SemaphoreType.DMA((2, 15)),
        ],
        compiler_params=pltpu.CompilerParams(
            collective_id=0, has_side_effects=True, vmem_limit_bytes=40 * 1024 * 1024
        ),
    )(coords.reshape(coords.shape[0]), blocks.reshape(slots * bi * bj, bk), factor_b, factor_c)


def solution(mesh):
    sizes = (mesh.shape["ia"], mesh.shape["ja"], mesh.shape["ka"])
    placed = (
        P(("ia", "ja", "ka"), None, None, None),
        P(None, ("ia", "ja", "ka")),
        P(("ia", "ja", "ka")),
        P("ja", None),
        P("ka", None),
    )
    return jax.shard_map(
        functools.partial(on_device, sizes),
        mesh=mesh,
        in_specs=placed,
        out_specs=(P("ia", None), P("ja", None), P("ka", None)),
        check_vma=False,
    )
```

```python
import functools

import jax
import jax.numpy as jnp
from jax import lax
from jax.experimental import pallas as pl
from jax.experimental.pallas import tpu as pltpu
from jax.sharding import PartitionSpec as P

GI_DEV = 4
RIDGE_SHARE = 0.3
EPSILON = 1e-06
HIGHEST = lax.Precision.HIGHEST
MESH = pl.DeviceIdType.MESH
F32 = jnp.float32
BF16 = jnp.bfloat16
CHUNK = 8


def newton_plan(order):
    low = RIDGE_SHARE / order
    high = 1.0 + low
    first = 2.0 / (low + high)
    error = (high - low) / (high + low)
    scales = []
    while error > 1e-9:
        square = error * error
        scales.append(2.0 / (2.0 - square))
        error = square / (2.0 - square)
    return first, scales


def dot_high(left, right):
    return jnp.dot(left, right, precision=HIGHEST, preferred_element_type=F32)


def halves(values):
    head = values.astype(BF16)
    return head, (values - head.astype(F32)).astype(BF16)


def dot_middle(left, right):
    left_head, left_tail = halves(left)
    right_head, right_tail = halves(right)

    def times(one, two):
        return jnp.dot(one, two, preferred_element_type=F32)

    return times(left_head, right_head) + (
        times(left_head, right_tail) + times(left_tail, right_head)
    )


def system_inverse(gram_one, gram_two):
    order = gram_one.shape[0]
    merged = gram_one * gram_two
    on_diagonal = lax.broadcasted_iota(jnp.int32, (order, order), 0) == lax.broadcasted_iota(
        jnp.int32, (order, order), 1
    )
    eye = jnp.where(on_diagonal, 1.0, 0.0).astype(F32)
    trace = jnp.sum(jnp.sum(merged * eye, axis=1, keepdims=True), axis=0, keepdims=True)
    unit = 1.0 / trace
    system = merged * unit + (RIDGE_SHARE / order) * eye
    first, scales = newton_plan(order)
    twice = 2.0 * eye
    start = scales[0] * first
    guess = start * (twice - first * system)
    image = start * (2.0 * system - first * dot_middle(system, system))
    for scale in scales[1:-2]:
        both = scale * dot_middle(jnp.concatenate([image, guess], axis=0), twice - image)
        image, guess = both[:order], both[order:]
    for scale, times in zip(scales[-2:], (dot_middle, dot_high)):
        guess = scale * times(guess, twice - times(system, guess))
    return guess * unit


def gram_of(values):
    return lax.dot_general(
        values, values, (((0,), (0,)), ((), ())), precision=HIGHEST, preferred_element_type=F32
    )


def kernel(
    sizes,
    coords,
    tensor_hbm,
    factor_b_hbm,
    factor_c_hbm,
    out_a,
    out_b,
    out_c,
    tensor,
    factor_b,
    factor_c,
    wide,
    turned,
    upright,
    rows_one,
    plane_b,
    slices_b,
    whole_b,
    gram_c_buf,
    plane_a_buf,
    plane_2,
    slices_2,
    whole_2,
    send_0,
    send_1,
    send_2,
    take_0,
    take_1,
    take_2,
    share_0,
    share_1,
    share_2,
    own_sums,
    sums_0,
    sums_1,
    sums_2,
    load_sems,
    sems,
):
    n_i, n_j, n_k = sizes
    n_all = n_i * n_j * n_k
    p, q, s = lax.axis_index("ia"), lax.axis_index("ja"), lax.axis_index("ka")
    spans = (out_a.shape[0], out_b.shape[0], out_c.shape[0])
    extents = (turned.shape[1], turned.shape[0], turned.shape[2])
    counts = tuple(span // extent for span, extent in zip(spans, extents))
    lengths = (spans[0] * n_i, spans[1] * n_j, spans[2] * n_k)
    rank = out_a.shape[1]

    loads = [
        pltpu.make_async_copy(source, target, load_sems.at[i])
        for i, (source, target) in enumerate(
            ((factor_b_hbm, factor_b), (factor_c_hbm, factor_c), (tensor_hbm, tensor))
        )
    ]
    for load in loads:
        load.start()

    position = (p, q, s)
    shifted = [
        [lax.rem(place + offset, size) for offset in range(size)]
        for place, size in zip(position, sizes)
    ]

    class Group:
        def __init__(self, *axes):
            self.axes = axes
            self.size = 1
            self.mine = 0
            for axis in axes:
                self.size *= sizes[axis]
                self.mine = self.mine * sizes[axis] + position[axis]

        def outside(self, body):
            (axis,) = (i for i in range(3) if i not in self.axes)

            def visit(step, index):
                device, rest, slot = list(position), index, (step - 1) * self.size + self.mine
                device[axis] = lax.rem(position[axis] + step, sizes[axis])
                for other in reversed(self.axes):
                    if isinstance(rest, int):
                        device[other] = shifted[other][rest % sizes[other]]
                    else:
                        device[other] = lax.rem(rest, sizes[other])
                    rest = rest // sizes[other]
                body(slot, tuple(device))

            for step in range(1, sizes[axis]):
                if self.size <= 16:
                    for index in range(self.size):
                        visit(step, index)
                else:
                    pl.loop(0, self.size)(functools.partial(visit, step))

        def partners(self, body):
            if self.size <= 32:
                for offset in range(1, self.size):
                    device, other, rest = list(position), 0, []
                    for axis in reversed(self.axes):
                        rest.append(offset % sizes[axis])
                        offset //= sizes[axis]
                    for axis, step in zip(self.axes, reversed(rest)):
                        device[axis] = shifted[axis][step]
                        other = other * sizes[axis] + device[axis]
                    body(other, tuple(device))
            else:

                @pl.loop(1, self.size)
                def _(offset):
                    other = lax.rem(self.mine + offset, self.size)
                    device, rest = list(position), other
                    for axis in reversed(self.axes):
                        device[axis] = lax.rem(rest, sizes[axis])
                        rest = rest // sizes[axis]
                    body(other, tuple(device))

    everyone = Group(0, 1, 2)
    groups = (Group(1, 2), Group(0, 2), Group(0, 1))
    lines = (Group(0), Group(1), Group(2))

    def copy(source, target, phase, device):
        return pltpu.make_async_remote_copy(
            src_ref=source,
            dst_ref=target,
            send_sem=sems.at[0, phase],
            recv_sem=sems.at[1, phase],
            device_id=device,
            device_id_type=MESH,
        )

    def all_but_one(group, buffer, phase):
        part = buffer.at[pl.ds(0, group.size - 1)]
        return copy(part, part, phase, tuple(row[-1] for row in shifted))

    def spread(group, buffer, phase):
        slot = buffer.at[group.mine]
        group.partners(lambda other, device: copy(slot, slot, phase, device).start())

    def deal(group, source, target, phase):
        group.partners(
            lambda other, device: copy(
                source.at[other], target.at[group.mine], phase, device
            ).start()
        )

    def arrive(group, buffer, phase):
        all_but_one(group, buffer, phase).wait_recv()

    def sent(group, buffer, phase):
        all_but_one(group, buffer, phase).wait_send()

    barrier = pltpu.get_barrier_semaphore()
    everyone.partners(
        lambda other, device: pl.semaphore_signal(
            barrier, inc=1, device_id=device, device_id_type=MESH
        )
    )

    def store_slices(gram, plane):
        share = plane.shape[1]
        for u in range(plane.shape[0]):
            plane[u] = gram[u * share : (u + 1) * share, :]

    def start_slices(gram, plane, slices, phase):
        store_slices(gram, plane)
        mine = plane.at[groups[1].mine]
        target = slices.at[q]
        lines[1].partners(lambda other, device: copy(mine, target, phase, device).start())

    def turn_slices(plane, slices, whole, phase):
        arrive(lines[1], slices, phase)
        slices[q] = plane[groups[1].mine]
        whole[groups[1].mine] = jnp.sum(slices[...], axis=0)
        spread(groups[1], whole, phase + 1)

    def end_slices(whole, phase):
        arrive(groups[1], whole, phase + 1)
        return whole[...].reshape(rank, rank) / lengths[1]

    loads[0].wait()
    first_gram_b = gram_of(factor_b[...])
    loads[1].wait()
    gram_c_buf[s] = gram_of(factor_c[...])
    pl.semaphore_wait(barrier, n_all - 1)
    start_slices(first_gram_b, plane_b, slices_b, 0)
    spread(lines[2], gram_c_buf, 2)

    def marks_of(mode, base):
        row = lax.broadcasted_iota(jnp.int32, (counts[mode], rank), 0) + base
        return jnp.where(row == jnp.full(row.shape, coords[mode], jnp.int32), 1.0, 0.0)

    marks = (marks_of(0, p * counts[0]), marks_of(1, q * counts[1]), marks_of(2, s * counts[2]))

    def block_rows(mode, source):
        extent = extents[mode]
        return sum(
            source[g * extent : (g + 1) * extent, :] * marks[mode][g : g + 1, :]
            for g in range(counts[mode])
        )

    loads[2].wait()
    wide[...] = tensor[...].astype(F32)

    @pl.loop(0, extents[1], unroll=8)
    def _(b):
        turned[b] = wide[pl.ds(b, extents[0], stride=extents[1]), :].astype(BF16)

    def product(mode, rows_of_one, rows_of_two):
        rows_one[0 : rows_of_one.shape[0], :] = rows_of_one
        total = jnp.zeros((extents[mode], rank), F32)

        def step(j, total):
            ones = rows_one[pl.ds(pl.multiple_of(j * CHUNK, CHUNK), CHUNK), :]
            khatri = jnp.concatenate(
                [(ones[i : i + 1, :] * rows_of_two).astype(BF16) for i in range(CHUNK)], axis=0
            )
            if mode == 2:
                depth = CHUNK * extents[1]
                left = upright[:, pl.ds(pl.multiple_of(j * depth, depth), depth)]
            else:
                if mode == 0:
                    parts = [turned[j * CHUNK + i] for i in range(CHUNK)]
                else:
                    height = extents[1]
                    parts = [
                        tensor[pl.ds(pl.multiple_of((j * CHUNK + i) * height, height), height), :]
                        for i in range(CHUNK)
                    ]
                left = jnp.concatenate(parts, axis=1)
            return total + jnp.dot(left, khatri, preferred_element_type=F32)

        return lax.fori_loop(0, rows_of_one.shape[0] // CHUNK, step, total, unroll=True)

    def cut(mode, rows, send, take, phase):
        group = groups[mode]
        share = extents[mode] // group.size
        for u in range(group.size):
            send[u, 0:share, :] = rows[u * share : (u + 1) * share, :]
            send[u, share : share + counts[mode], :] = marks[mode]
        deal(group, send, take, phase)

    def gather_cut(mode, send, take, phase):
        group = groups[mode]
        share, count = extents[mode] // group.size, counts[mode]
        arrive(group, take, phase)
        take[group.mine] = send[group.mine]
        total = [jnp.zeros((share, rank), F32) for _ in range(count)]
        for u in range(group.size):
            rows = take[u, 0:share, :]
            for g in range(count):
                total[g] = total[g] + rows * take[u, share + g : share + g + 1, :]
        return jnp.concatenate(total, axis=0)

    def settle(mode, send, take, inverse, shares, sums, out, phase, meanwhile=None):
        group = groups[mode]
        share = extents[mode] // group.size
        solved = dot_high(gather_cut(mode, send, take, phase), inverse)
        shares[group.mine] = solved
        spread(group, shares, phase + 2)
        own_sums[mode] = jnp.sum(solved * solved, axis=0, keepdims=True)
        group.outside(
            lambda slot, device: copy(
                own_sums.at[mode], sums.at[slot], phase + 1, device
            ).start()
        )
        if meanwhile is not None:
            meanwhile()
        copy(sums, sums, phase + 1, position).wait_recv()
        arrive(group, shares, phase + 2)
        squares = jnp.sum(sums[...], axis=0)
        for u in range(group.size):
            squares = squares + jnp.sum(shares[u] * shares[u], axis=0, keepdims=True)
        squares = squares / lengths[mode]
        scale = lax.rsqrt(squares + EPSILON)
        for u in range(group.size):
            rows = shares[u] * scale
            for g in range(counts[mode]):
                start = g * extents[mode] + u * share
                out[start : start + share, :] = rows[g * share : (g + 1) * share, :]

    def stand_up():
        depth = CHUNK * extents[1]
        for start in range(0, tensor.shape[0], depth):
            upright[:, start : start + depth] = tensor[start : start + depth, :].T

    rows = product(0, block_rows(1, factor_b), block_rows(2, factor_c))
    cut(0, rows, send_0, take_0, 3)
    turn_slices(plane_b, slices_b, whole_b, 0)
    arrive(lines[2], gram_c_buf, 2)
    gram_c = jnp.sum(gram_c_buf[...], axis=0) / lengths[2]
    gram_b = end_slices(whole_b, 0)
    inverse = system_inverse(gram_b, gram_c)
    settle(0, send_0, take_0, inverse, share_0, sums_0, out_a, 3, stand_up)
    plane_a_buf[p] = gram_of(out_a[...])
    spread(lines[0], plane_a_buf, 6)

    rows = product(1, block_rows(0, out_a), block_rows(2, factor_c))
    cut(1, rows, send_1, take_1, 7)
    arrive(lines[0], plane_a_buf, 6)
    gram_a = jnp.sum(plane_a_buf[...], axis=0) / lengths[0]
    inverse = system_inverse(gram_a, gram_c)
    settle(1, send_1, take_1, inverse, share_1, sums_1, out_b, 7)
    start_slices(gram_of(out_b[...]), plane_2, slices_2, 10)

    rows = product(2, block_rows(0, out_a), block_rows(1, out_b))
    turn_slices(plane_2, slices_2, whole_2, 10)
    cut(2, rows, send_2, take_2, 12)
    gram_b = end_slices(whole_2, 10)
    inverse = system_inverse(gram_a, gram_b)
    settle(2, send_2, take_2, inverse, share_2, sums_2, out_c, 12)

    sent(lines[1], slices_b, 0)
    sent(groups[1], whole_b, 1)
    sent(lines[2], gram_c_buf, 2)
    sent(groups[0], send_0, 3)
    copy(sums_0, sums_0, 4, position).wait_send()
    sent(groups[0], share_0, 5)
    sent(lines[0], plane_a_buf, 6)
    sent(groups[1], send_1, 7)
    copy(sums_1, sums_1, 8, position).wait_send()
    sent(groups[1], share_1, 9)
    sent(lines[1], slices_2, 10)
    sent(groups[1], whole_2, 11)
    sent(groups[2], send_2, 12)
    copy(sums_2, sums_2, 13, position).wait_send()
    sent(groups[2], share_2, 14)


def store_kernel(one, two, three, out_one, out_two, out_three, sems):
    copies = [
        pltpu.make_async_copy(source, target, sems.at[i])
        for i, (source, target) in enumerate(((one, out_one), (two, out_two), (three, out_three)))
    ]
    for copy in copies:
        copy.start()
    for copy in copies:
        copy.wait()


def on_device(sizes, blocks, coords, live, factor_b, factor_c):
    n_i, n_j, n_k = sizes
    n_all = n_i * n_j * n_k
    slots, bi, bj, bk = blocks.shape
    rank = factor_b.shape[1]
    group_sizes = (n_j * n_k, n_i * n_k, n_i * n_j)
    spans = (GI_DEV * bi, factor_b.shape[0], factor_c.shape[0])
    extents = (bi, bj, bk)

    def message(mode):
        rows = extents[mode] // group_sizes[mode] + spans[mode] // extents[mode]
        return (group_sizes[mode], (rows + 7) // 8 * 8, rank)

    def buffer(*shape):
        return pltpu.VMEM(shape, F32)

    slices = [
        buffer(group_sizes[1], rank // group_sizes[1], rank),
        buffer(n_j, rank // group_sizes[1], rank),
        buffer(group_sizes[1], rank // group_sizes[1], rank),
    ]
    vmem = pl.BlockSpec(memory_space=pltpu.VMEM)
    far = pl.BlockSpec(memory_space=pltpu.HBM)
    shapes = [jax.ShapeDtypeStruct((span, rank), F32) for span in spans]
    factors = pl.pallas_call(
        functools.partial(kernel, sizes),
        out_shape=shapes,
        in_specs=[pl.BlockSpec(memory_space=pltpu.SMEM), far, far, far],
        out_specs=[vmem] * 3,
        scratch_shapes=[
            pltpu.VMEM((bi * bj, bk), BF16),
            buffer(*factor_b.shape),
            buffer(*factor_c.shape),
            buffer(bi * bj, bk),
            pltpu.VMEM((bj, bi, bk), BF16),
            pltpu.VMEM((bk, bi * bj), BF16),
            buffer(max(bi, bj), rank),
            *slices,
            buffer(n_k, rank, rank),
            buffer(n_i, rank, rank),
            *slices,
            *[buffer(*message(mode)) for mode in range(3)],
            *[buffer(*message(mode)) for mode in range(3)],
            *[buffer(group_sizes[mode], spans[mode] // group_sizes[mode], rank) for mode in range(3)],
            buffer(3, 1, rank),
            *[buffer(n_all - size, 1, rank) for size in group_sizes],
            pltpu.SemaphoreType.DMA((3,)),
            pltpu.SemaphoreType.DMA((2, 15)),
        ],
        compiler_params=pltpu.CompilerParams(
            collective_id=0, has_side_effects=True, vmem_limit_bytes=48 * 1024 * 1024
        ),
    )(coords.reshape(coords.shape[0]), blocks.reshape(slots * bi * bj, bk), factor_b, factor_c)
    return pl.pallas_call(
        store_kernel,
        out_shape=shapes,
        in_specs=[pl.BlockSpec(memory_space=pl.ANY)] * 3,
        out_specs=[far] * 3,
        scratch_shapes=[pltpu.SemaphoreType.DMA((3,))],
    )(*factors)


def solution(mesh):
    sizes = (mesh.shape["ia"], mesh.shape["ja"], mesh.shape["ka"])
    placed = (
        P(("ia", "ja", "ka"), None, None, None),
        P(None, ("ia", "ja", "ka")),
        P(("ia", "ja", "ka")),
        P("ja", None),
        P("ka", None),
    )
    return jax.shard_map(
        functools.partial(on_device, sizes),
        mesh=mesh,
        in_specs=placed,
        out_specs=(P("ia", None), P("ja", None), P("ka", None)),
        check_vma=False,
    )
```

```python
import functools

import jax
import jax.numpy as jnp
from jax import lax
from jax.experimental import pallas as pl
from jax.experimental.pallas import tpu as pltpu
from jax.sharding import PartitionSpec as P

GI_DEV = 4
RIDGE_SHARE = 0.3
EPSILON = 1e-06
HIGHEST = lax.Precision.HIGHEST
MESH = pl.DeviceIdType.MESH
F32 = jnp.float32
BF16 = jnp.bfloat16
CHUNK = 8


def newton_plan(order):
    low = RIDGE_SHARE / order
    high = 1.0 + low
    first = 2.0 / (low + high)
    error = (high - low) / (high + low)
    scales = []
    while error > 1e-9:
        square = error * error
        scales.append(2.0 / (2.0 - square))
        error = square / (2.0 - square)
    return first, scales


def dot_high(left, right):
    return jnp.dot(left, right, precision=HIGHEST, preferred_element_type=F32)


def halves(values):
    head = values.astype(BF16)
    return head, (values - head.astype(F32)).astype(BF16)


def dot_middle(left, right):
    left_head, left_tail = halves(left)
    right_head, right_tail = halves(right)

    def times(one, two):
        return jnp.dot(one, two, preferred_element_type=F32)

    return times(left_head, right_head) + (
        times(left_head, right_tail) + times(left_tail, right_head)
    )


def system_inverse(gram_one, gram_two):
    order = gram_one.shape[0]
    merged = gram_one * gram_two
    on_diagonal = lax.broadcasted_iota(jnp.int32, (order, order), 0) == lax.broadcasted_iota(
        jnp.int32, (order, order), 1
    )
    eye = jnp.where(on_diagonal, 1.0, 0.0).astype(F32)
    trace = jnp.sum(jnp.sum(merged * eye, axis=1, keepdims=True), axis=0, keepdims=True)
    unit = 1.0 / trace
    system = merged * unit + (RIDGE_SHARE / order) * eye
    first, scales = newton_plan(order)
    twice = 2.0 * eye
    start = scales[0] * first
    guess = start * (twice - first * system)
    image = start * (2.0 * system - first * dot_middle(system, system))
    for scale in scales[1:-1]:
        both = scale * dot_middle(jnp.concatenate([image, guess], axis=0), twice - image)
        image, guess = both[:order], both[order:]
    guess = scales[-1] * dot_high(guess, twice - dot_high(system, guess))
    return guess * unit


def gram_of(values):
    return lax.dot_general(
        values, values, (((0,), (0,)), ((), ())), precision=HIGHEST, preferred_element_type=F32
    )


def kernel(
    sizes,
    coords,
    tensor_hbm,
    factor_b_hbm,
    factor_c_hbm,
    out_a,
    out_b,
    out_c,
    tensor,
    factor_b,
    factor_c,
    wide,
    turned,
    upright,
    rows_one,
    plane_b,
    slices_b,
    whole_b,
    gram_c_buf,
    plane_a_buf,
    plane_2,
    slices_2,
    whole_2,
    send_0,
    send_1,
    send_2,
    take_0,
    take_1,
    take_2,
    share_0,
    share_1,
    share_2,
    own_sums,
    sums_0,
    sums_1,
    sums_2,
    load_sems,
    sems,
    line_sems,
):
    n_i, n_j, n_k = sizes
    n_all = n_i * n_j * n_k
    p, q, s = lax.axis_index("ia"), lax.axis_index("ja"), lax.axis_index("ka")
    spans = (out_a.shape[0], out_b.shape[0], out_c.shape[0])
    extents = (turned.shape[1], turned.shape[0], turned.shape[2])
    counts = tuple(span // extent for span, extent in zip(spans, extents))
    lengths = (spans[0] * n_i, spans[1] * n_j, spans[2] * n_k)
    rank = out_a.shape[1]

    loads = [
        pltpu.make_async_copy(source, target, load_sems.at[i])
        for i, (source, target) in enumerate(
            ((factor_b_hbm, factor_b), (factor_c_hbm, factor_c), (tensor_hbm, tensor))
        )
    ]
    for load in loads:
        load.start()

    position = (p, q, s)
    shifted = [
        [lax.rem(place + offset, size) for offset in range(size)]
        for place, size in zip(position, sizes)
    ]

    class Group:
        def __init__(self, *axes):
            self.axes = axes
            self.size = 1
            self.mine = 0
            for axis in axes:
                self.size *= sizes[axis]
                self.mine = self.mine * sizes[axis] + position[axis]

        def outside(self, body):
            (axis,) = (i for i in range(3) if i not in self.axes)

            def visit(step, index):
                device, rest, slot = list(position), index, (step - 1) * self.size + self.mine
                device[axis] = lax.rem(position[axis] + step, sizes[axis])
                for other in reversed(self.axes):
                    if isinstance(rest, int):
                        device[other] = shifted[other][rest % sizes[other]]
                    else:
                        device[other] = lax.rem(rest, sizes[other])
                    rest = rest // sizes[other]
                body(slot, tuple(device))

            for step in range(1, sizes[axis]):
                if self.size <= 16:
                    for index in range(self.size):
                        visit(step, index)
                else:
                    pl.loop(0, self.size)(functools.partial(visit, step))

        def partners(self, body):
            if self.size <= 32:
                for offset in range(1, self.size):
                    device, other, rest = list(position), 0, []
                    for axis in reversed(self.axes):
                        rest.append(offset % sizes[axis])
                        offset //= sizes[axis]
                    for axis, step in zip(self.axes, reversed(rest)):
                        device[axis] = shifted[axis][step]
                        other = other * sizes[axis] + device[axis]
                    body(other, tuple(device))
            else:

                @pl.loop(1, self.size)
                def _(offset):
                    other = lax.rem(self.mine + offset, self.size)
                    device, rest = list(position), other
                    for axis in reversed(self.axes):
                        device[axis] = lax.rem(rest, sizes[axis])
                        rest = rest // sizes[axis]
                    body(other, tuple(device))

    everyone = Group(0, 1, 2)
    groups = (Group(1, 2), Group(0, 2), Group(0, 1))
    lines = (Group(0), Group(1), Group(2))

    def copy(source, target, phase, device):
        return pltpu.make_async_remote_copy(
            src_ref=source,
            dst_ref=target,
            send_sem=sems.at[0, phase],
            recv_sem=sems.at[1, phase],
            device_id=device,
            device_id_type=MESH,
        )

    def all_but_one(group, buffer, phase):
        part = buffer.at[pl.ds(0, group.size - 1)]
        return copy(part, part, phase, tuple(row[-1] for row in shifted))

    def spread(group, buffer, phase):
        slot = buffer.at[group.mine]
        group.partners(lambda other, device: copy(slot, slot, phase, device).start())

    def deal(group, source, target, phase):
        group.partners(
            lambda other, device: copy(
                source.at[other], target.at[group.mine], phase, device
            ).start()
        )

    def arrive(group, buffer, phase):
        all_but_one(group, buffer, phase).wait_recv()

    def sent(group, buffer, phase):
        all_but_one(group, buffer, phase).wait_send()

    barrier = pltpu.get_barrier_semaphore()
    everyone.partners(
        lambda other, device: pl.semaphore_signal(
            barrier, inc=1, device_id=device, device_id_type=MESH
        )
    )

    def store_slices(gram, plane):
        share = plane.shape[1]
        for u in range(plane.shape[0]):
            plane[u] = gram[u * share : (u + 1) * share, :]

    def start_slices(gram, plane, slices, phase):
        store_slices(gram, plane)
        mine = plane.at[groups[1].mine]
        target = slices.at[q]
        lines[1].partners(lambda other, device: copy(mine, target, phase, device).start())

    def turn_slices(plane, slices, whole, phase):
        arrive(lines[1], slices, phase)
        slices[q] = plane[groups[1].mine]
        whole[groups[1].mine] = jnp.sum(slices[...], axis=0)
        spread(groups[1], whole, phase + 1)

    def end_slices(whole, phase):
        arrive(groups[1], whole, phase + 1)
        return whole[...].reshape(rank, rank) / lengths[1]

    loads[0].wait()
    first_gram_b = gram_of(factor_b[...])
    loads[1].wait()
    gram_c_buf[s] = gram_of(factor_c[...])
    pl.semaphore_wait(barrier, n_all - 1)
    start_slices(first_gram_b, plane_b, slices_b, 0)
    spread(lines[2], gram_c_buf, 2)

    def marks_of(mode, base):
        row = lax.broadcasted_iota(jnp.int32, (counts[mode], rank), 0) + base
        return jnp.where(row == jnp.full(row.shape, coords[mode], jnp.int32), 1.0, 0.0)

    marks = (marks_of(0, p * counts[0]), marks_of(1, q * counts[1]), marks_of(2, s * counts[2]))

    def block_rows(mode, source):
        extent = extents[mode]
        return sum(
            source[g * extent : (g + 1) * extent, :] * marks[mode][g : g + 1, :]
            for g in range(counts[mode])
        )

    loads[2].wait()
    wide[...] = tensor[...].astype(F32)

    @pl.loop(0, extents[1], unroll=8)
    def _(b):
        turned[b] = wide[pl.ds(b, extents[0], stride=extents[1]), :].astype(BF16)

    def product(mode, rows_of_one, rows_of_two):
        rows_one[0 : rows_of_one.shape[0], :] = rows_of_one
        total = jnp.zeros((extents[mode], rank), F32)

        def step(j, total):
            ones = rows_one[pl.ds(pl.multiple_of(j * CHUNK, CHUNK), CHUNK), :]
            khatri = jnp.concatenate(
                [(ones[i : i + 1, :] * rows_of_two).astype(BF16) for i in range(CHUNK)], axis=0
            )
            if mode == 2:
                depth = CHUNK * extents[1]
                left = upright[:, pl.ds(pl.multiple_of(j * depth, depth), depth)]
            else:
                if mode == 0:
                    parts = [turned[j * CHUNK + i] for i in range(CHUNK)]
                else:
                    height = extents[1]
                    parts = [
                        tensor[pl.ds(pl.multiple_of((j * CHUNK + i) * height, height), height), :]
                        for i in range(CHUNK)
                    ]
                left = jnp.concatenate(parts, axis=1)
            return total + jnp.dot(left, khatri, preferred_element_type=F32)

        return lax.fori_loop(0, rows_of_one.shape[0] // CHUNK, step, total, unroll=True)

    def cut(mode, rows, send, take, phase):
        group = groups[mode]
        share = extents[mode] // group.size
        for u in range(group.size):
            send[u, 0:share, :] = rows[u * share : (u + 1) * share, :]
            send[u, share : share + counts[mode], :] = marks[mode]
        deal(group, send, take, phase)

    def gather_cut(mode, send, take, phase):
        group = groups[mode]
        share, count = extents[mode] // group.size, counts[mode]
        arrive(group, take, phase)
        take[group.mine] = send[group.mine]
        total = [jnp.zeros((share, rank), F32) for _ in range(count)]
        for u in range(group.size):
            rows = take[u, 0:share, :]
            for g in range(count):
                total[g] = total[g] + rows * take[u, share + g : share + g + 1, :]
        return jnp.concatenate(total, axis=0)

    def line_copy(group, buffer, step, column):
        slot = buffer.at[p * n_j + column]
        return pltpu.make_async_remote_copy(
            src_ref=slot,
            dst_ref=slot,
            send_sem=line_sems.at[0, step],
            recv_sem=line_sems.at[1, step],
            device_id=(p, shifted[1][step], s),
            device_id_type=MESH,
        )

    def start_relay(group, buffer, phase):
        for step in range(1, n_j):
            line_copy(group, buffer, step, q).start()
        slot = buffer.at[group.mine]
        lines[0].partners(lambda other, device: copy(slot, slot, phase, device).start())

    def end_relay(group, buffer, phase):
        for step in range(1, n_j):
            column = shifted[1][n_j - step]
            line_copy(group, buffer, step, column).wait_recv()
            slot = buffer.at[p * n_j + column]
            lines[0].partners(
                lambda other, device, slot=slot: copy(slot, slot, phase, device).start()
            )
        copy(*[buffer.at[pl.ds(0, (n_i - 1) * n_j)]] * 2, phase, position).wait_recv()

    def settle(mode, send, take, inverse, shares, sums, out, phase, meanwhile=None, relay=False):
        group = groups[mode]
        share = extents[mode] // group.size
        solved = dot_high(gather_cut(mode, send, take, phase), inverse)
        shares[group.mine] = solved
        if relay:
            start_relay(group, shares, phase + 2)
        else:
            spread(group, shares, phase + 2)
        own_sums[mode] = jnp.sum(solved * solved, axis=0, keepdims=True)
        group.outside(
            lambda slot, device: copy(
                own_sums.at[mode], sums.at[slot], phase + 1, device
            ).start()
        )
        if meanwhile is not None:
            meanwhile()
        if relay:
            end_relay(group, shares, phase + 2)
        else:
            arrive(group, shares, phase + 2)
        copy(sums, sums, phase + 1, position).wait_recv()
        squares = jnp.sum(sums[...], axis=0)
        for u in range(group.size):
            squares = squares + jnp.sum(shares[u] * shares[u], axis=0, keepdims=True)
        squares = squares / lengths[mode]
        scale = lax.rsqrt(squares + EPSILON)
        for u in range(group.size):
            rows = shares[u] * scale
            for g in range(counts[mode]):
                start = g * extents[mode] + u * share
                out[start : start + share, :] = rows[g * share : (g + 1) * share, :]

    def stand_up():
        depth = CHUNK * extents[1]
        for start in range(0, tensor.shape[0], depth):
            upright[:, start : start + depth] = tensor[start : start + depth, :].T

    rows = product(0, block_rows(1, factor_b), block_rows(2, factor_c))
    cut(0, rows, send_0, take_0, 3)
    turn_slices(plane_b, slices_b, whole_b, 0)
    arrive(lines[2], gram_c_buf, 2)
    gram_c = jnp.sum(gram_c_buf[...], axis=0) / lengths[2]
    gram_b = end_slices(whole_b, 0)
    inverse = system_inverse(gram_b, gram_c)
    settle(0, send_0, take_0, inverse, share_0, sums_0, out_a, 3, stand_up)
    plane_a_buf[p] = gram_of(out_a[...])
    spread(lines[0], plane_a_buf, 6)

    rows = product(1, block_rows(0, out_a), block_rows(2, factor_c))
    cut(1, rows, send_1, take_1, 7)
    arrive(lines[0], plane_a_buf, 6)
    gram_a = jnp.sum(plane_a_buf[...], axis=0) / lengths[0]
    inverse = system_inverse(gram_a, gram_c)
    settle(1, send_1, take_1, inverse, share_1, sums_1, out_b, 7)
    start_slices(gram_of(out_b[...]), plane_2, slices_2, 10)

    rows = product(2, block_rows(0, out_a), block_rows(1, out_b))
    turn_slices(plane_2, slices_2, whole_2, 10)
    cut(2, rows, send_2, take_2, 12)
    gram_b = end_slices(whole_2, 10)
    inverse = system_inverse(gram_a, gram_b)
    settle(2, send_2, take_2, inverse, share_2, sums_2, out_c, 12, relay=True)

    sent(lines[1], slices_b, 0)
    sent(groups[1], whole_b, 1)
    sent(lines[2], gram_c_buf, 2)
    sent(groups[0], send_0, 3)
    copy(sums_0, sums_0, 4, position).wait_send()
    sent(groups[0], share_0, 5)
    sent(lines[0], plane_a_buf, 6)
    sent(groups[1], send_1, 7)
    copy(sums_1, sums_1, 8, position).wait_send()
    sent(groups[1], share_1, 9)
    sent(lines[1], slices_2, 10)
    sent(groups[1], whole_2, 11)
    sent(groups[2], send_2, 12)
    copy(sums_2, sums_2, 13, position).wait_send()
    for step in range(1, n_j):
        line_copy(groups[2], share_2, step, q).wait_send()
    copy(*[share_2.at[pl.ds(0, (n_i - 1) * n_j)]] * 2, 14, position).wait_send()


def on_device(sizes, blocks, coords, live, factor_b, factor_c):
    n_i, n_j, n_k = sizes
    n_all = n_i * n_j * n_k
    slots, bi, bj, bk = blocks.shape
    rank = factor_b.shape[1]
    group_sizes = (n_j * n_k, n_i * n_k, n_i * n_j)
    spans = (GI_DEV * bi, factor_b.shape[0], factor_c.shape[0])
    extents = (bi, bj, bk)

    def message(mode):
        rows = extents[mode] // group_sizes[mode] + spans[mode] // extents[mode]
        return (group_sizes[mode], (rows + 7) // 8 * 8, rank)

    def buffer(*shape):
        return pltpu.VMEM(shape, F32)

    slices = [
        buffer(group_sizes[1], rank // group_sizes[1], rank),
        buffer(n_j, rank // group_sizes[1], rank),
        buffer(group_sizes[1], rank // group_sizes[1], rank),
    ]
    vmem = pl.BlockSpec(memory_space=pltpu.VMEM)
    far = pl.BlockSpec(memory_space=pltpu.HBM)
    shapes = [jax.ShapeDtypeStruct((span, rank), F32) for span in spans]
    return pl.pallas_call(
        functools.partial(kernel, sizes),
        out_shape=shapes,
        in_specs=[pl.BlockSpec(memory_space=pltpu.SMEM), far, far, far],
        out_specs=[vmem] * 3,
        scratch_shapes=[
            pltpu.VMEM((bi * bj, bk), BF16),
            buffer(*factor_b.shape),
            buffer(*factor_c.shape),
            buffer(bi * bj, bk),
            pltpu.VMEM((bj, bi, bk), BF16),
            pltpu.VMEM((bk, bi * bj), BF16),
            buffer(max(bi, bj), rank),
            *slices,
            buffer(n_k, rank, rank),
            buffer(n_i, rank, rank),
            *slices,
            *[buffer(*message(mode)) for mode in range(3)],
            *[buffer(*message(mode)) for mode in range(3)],
            *[buffer(group_sizes[mode], spans[mode] // group_sizes[mode], rank) for mode in range(3)],
            buffer(3, 1, rank),
            *[buffer(n_all - size, 1, rank) for size in group_sizes],
            pltpu.SemaphoreType.DMA((3,)),
            pltpu.SemaphoreType.DMA((2, 15)),
            pltpu.SemaphoreType.DMA((2, n_j)),
        ],
        compiler_params=pltpu.CompilerParams(
            collective_id=0, has_side_effects=True, vmem_limit_bytes=48 * 1024 * 1024
        ),
    )(
        coords.reshape(coords.shape[0]),
        *(
            pltpu.with_memory_space_constraint(array, pltpu.HBM)
            for array in (blocks.reshape(slots * bi * bj, bk), factor_b, factor_c)
        ),
    )


def solution(mesh):
    sizes = (mesh.shape["ia"], mesh.shape["ja"], mesh.shape["ka"])
    placed = (
        P(("ia", "ja", "ka"), None, None, None),
        P(None, ("ia", "ja", "ka")),
        P(("ia", "ja", "ka")),
        P("ja", None),
        P("ka", None),
    )
    return jax.shard_map(
        functools.partial(on_device, sizes),
        mesh=mesh,
        in_specs=placed,
        out_specs=(P("ia", None), P("ja", None), P("ka", None)),
        check_vma=False,
    )
```

```python
import functools

import jax
import jax.numpy as jnp
from jax import lax
from jax.experimental import pallas as pl
from jax.experimental.pallas import tpu as pltpu
from jax.sharding import PartitionSpec as P

GI_DEV = 4
RIDGE_SHARE = 0.3
EPSILON = 1e-06
HIGHEST = lax.Precision.HIGHEST
MESH = pl.DeviceIdType.MESH
F32 = jnp.float32
BF16 = jnp.bfloat16
CHUNK = 8


def newton_plan(order):
    low = RIDGE_SHARE / order
    high = 1.0 + low
    first = 2.0 / (low + high)
    error = (high - low) / (high + low)
    scales = []
    while error > 1e-9:
        square = error * error
        scales.append(2.0 / (2.0 - square))
        error = square / (2.0 - square)
    return first, scales


def dot_high(left, right):
    return jnp.dot(left, right, precision=HIGHEST, preferred_element_type=F32)


def halves(values):
    head = values.astype(BF16)
    return head, (values - head.astype(F32)).astype(BF16)


def dot_middle(left, right):
    left_head, left_tail = halves(left)
    right_head, right_tail = halves(right)

    def times(one, two):
        return jnp.dot(one, two, preferred_element_type=F32)

    return times(left_head, right_head) + (
        times(left_head, right_tail) + times(left_tail, right_head)
    )


def system_inverse(gram_one, gram_two):
    order = gram_one.shape[0]
    merged = gram_one * gram_two
    on_diagonal = lax.broadcasted_iota(jnp.int32, (order, order), 0) == lax.broadcasted_iota(
        jnp.int32, (order, order), 1
    )
    eye = jnp.where(on_diagonal, 1.0, 0.0).astype(F32)
    trace = jnp.sum(jnp.sum(merged * eye, axis=1, keepdims=True), axis=0, keepdims=True)
    unit = 1.0 / trace
    system = merged * unit + (RIDGE_SHARE / order) * eye
    first, scales = newton_plan(order)
    twice = 2.0 * eye
    start = scales[0] * first
    guess = start * (twice - first * system)
    image = start * (2.0 * system - first * dot_middle(system, system))
    for scale in scales[1:-1]:
        both = scale * dot_middle(jnp.concatenate([image, guess], axis=0), twice - image)
        image, guess = both[:order], both[order:]
    guess = scales[-1] * dot_high(guess, twice - dot_high(system, guess))
    return guess * unit


def gram_of(values):
    return lax.dot_general(
        values, values, (((0,), (0,)), ((), ())), precision=HIGHEST, preferred_element_type=F32
    )


def kernel(
    sizes,
    coords,
    tensor_hbm,
    factor_b_hbm,
    factor_c_hbm,
    out_a,
    out_b,
    out_c,
    tensor,
    factor_b,
    factor_c,
    wide,
    turned,
    upright,
    rows_one,
    plane_b,
    slices_b,
    whole_b,
    gram_c_buf,
    plane_a_buf,
    plane_2,
    slices_2,
    whole_2,
    send_0,
    send_1,
    send_2,
    take_0,
    take_1,
    take_2,
    share_0,
    share_1,
    share_2,
    sums_0,
    sums_1,
    sums_2,
    load_sems,
    sems,
    line_sems,
):
    n_i, n_j, n_k = sizes
    n_all = n_i * n_j * n_k
    p, q, s = lax.axis_index("ia"), lax.axis_index("ja"), lax.axis_index("ka")
    spans = (out_a.shape[0], out_b.shape[0], out_c.shape[0])
    extents = (turned.shape[1], turned.shape[0], turned.shape[2])
    counts = tuple(span // extent for span, extent in zip(spans, extents))
    lengths = (spans[0] * n_i, spans[1] * n_j, spans[2] * n_k)
    rank = out_a.shape[1]

    loads = [
        pltpu.make_async_copy(source, target, load_sems.at[i])
        for i, (source, target) in enumerate(
            ((factor_b_hbm, factor_b), (factor_c_hbm, factor_c), (tensor_hbm, tensor))
        )
    ]
    for load in loads:
        load.start()

    position = (p, q, s)
    shifted = [
        [lax.rem(place + offset, size) for offset in range(size)]
        for place, size in zip(position, sizes)
    ]

    class Group:
        def __init__(self, *axes):
            self.axes = axes
            self.size = 1
            self.mine = 0
            for axis in axes:
                self.size *= sizes[axis]
                self.mine = self.mine * sizes[axis] + position[axis]

        def partners(self, body):
            if self.size <= 32:
                for offset in range(1, self.size):
                    device, other, rest = list(position), 0, []
                    for axis in reversed(self.axes):
                        rest.append(offset % sizes[axis])
                        offset //= sizes[axis]
                    for axis, step in zip(self.axes, reversed(rest)):
                        device[axis] = shifted[axis][step]
                        other = other * sizes[axis] + device[axis]
                    body(other, tuple(device))
            else:

                @pl.loop(1, self.size)
                def _(offset):
                    other = lax.rem(self.mine + offset, self.size)
                    device, rest = list(position), other
                    for axis in reversed(self.axes):
                        device[axis] = lax.rem(rest, sizes[axis])
                        rest = rest // sizes[axis]
                    body(other, tuple(device))

    everyone = Group(0, 1, 2)
    groups = (Group(1, 2), Group(0, 2), Group(0, 1))
    lines = (Group(0), Group(1), Group(2))

    def copy(source, target, phase, device):
        return pltpu.make_async_remote_copy(
            src_ref=source,
            dst_ref=target,
            send_sem=sems.at[0, phase],
            recv_sem=sems.at[1, phase],
            device_id=device,
            device_id_type=MESH,
        )

    def all_but_one(group, buffer, phase):
        part = buffer.at[pl.ds(0, group.size - 1)]
        return copy(part, part, phase, tuple(row[-1] for row in shifted))

    def spread(group, buffer, phase):
        slot = buffer.at[group.mine]
        group.partners(lambda other, device: copy(slot, slot, phase, device).start())

    def deal(group, source, target, phase):
        group.partners(
            lambda other, device: copy(
                source.at[other], target.at[group.mine], phase, device
            ).start()
        )

    def arrive(group, buffer, phase):
        all_but_one(group, buffer, phase).wait_recv()

    def sent(group, buffer, phase):
        all_but_one(group, buffer, phase).wait_send()

    barrier = pltpu.get_barrier_semaphore()
    everyone.partners(
        lambda other, device: pl.semaphore_signal(
            barrier, inc=1, device_id=device, device_id_type=MESH
        )
    )

    def store_slices(gram, plane):
        share = plane.shape[1]
        for u in range(plane.shape[0]):
            plane[u] = gram[u * share : (u + 1) * share, :]

    def start_slices(gram, plane, slices, phase):
        store_slices(gram, plane)
        mine = plane.at[groups[1].mine]
        target = slices.at[q]
        lines[1].partners(lambda other, device: copy(mine, target, phase, device).start())

    def turn_slices(plane, slices, whole, phase):
        arrive(lines[1], slices, phase)
        slices[q] = plane[groups[1].mine]
        whole[groups[1].mine] = jnp.sum(slices[...], axis=0)
        spread(groups[1], whole, phase + 1)

    def end_slices(whole, phase):
        arrive(groups[1], whole, phase + 1)
        return whole[...].reshape(rank, rank) / lengths[1]

    loads[0].wait()
    first_gram_b = gram_of(factor_b[...])
    loads[1].wait()
    gram_c_buf[s] = gram_of(factor_c[...])
    pl.semaphore_wait(barrier, n_all - 1)
    start_slices(first_gram_b, plane_b, slices_b, 0)
    spread(lines[2], gram_c_buf, 2)

    def marks_of(mode, base):
        row = lax.broadcasted_iota(jnp.int32, (counts[mode], rank), 0) + base
        return jnp.where(row == jnp.full(row.shape, coords[mode], jnp.int32), 1.0, 0.0)

    marks = (marks_of(0, p * counts[0]), marks_of(1, q * counts[1]), marks_of(2, s * counts[2]))

    def block_rows(mode, source):
        extent = extents[mode]
        return sum(
            source[g * extent : (g + 1) * extent, :] * marks[mode][g : g + 1, :]
            for g in range(counts[mode])
        )

    loads[2].wait()
    wide[...] = tensor[...].astype(F32)

    @pl.loop(0, extents[1], unroll=8)
    def _(b):
        turned[b] = wide[pl.ds(b, extents[0], stride=extents[1]), :].astype(BF16)

    def product(mode, rows_of_one, rows_of_two):
        rows_one[0 : rows_of_one.shape[0], :] = rows_of_one
        total = jnp.zeros((extents[mode], rank), F32)

        def step(j, total):
            ones = rows_one[pl.ds(pl.multiple_of(j * CHUNK, CHUNK), CHUNK), :]
            khatri = jnp.concatenate(
                [(ones[i : i + 1, :] * rows_of_two).astype(BF16) for i in range(CHUNK)], axis=0
            )
            if mode == 2:
                depth = CHUNK * extents[1]
                left = upright[:, pl.ds(pl.multiple_of(j * depth, depth), depth)]
            else:
                if mode == 0:
                    parts = [turned[j * CHUNK + i] for i in range(CHUNK)]
                else:
                    height = extents[1]
                    parts = [
                        tensor[pl.ds(pl.multiple_of((j * CHUNK + i) * height, height), height), :]
                        for i in range(CHUNK)
                    ]
                left = jnp.concatenate(parts, axis=1)
            return total + jnp.dot(left, khatri, preferred_element_type=F32)

        return lax.fori_loop(0, rows_of_one.shape[0] // CHUNK, step, total, unroll=True)

    def cut(mode, rows, send, take, phase):
        group = groups[mode]
        share = extents[mode] // group.size
        for u in range(group.size):
            send[u, 0:share, :] = rows[u * share : (u + 1) * share, :]
            send[u, share : share + counts[mode], :] = marks[mode]
        deal(group, send, take, phase)

    def gather_cut(mode, send, take, phase):
        group = groups[mode]
        share, count = extents[mode] // group.size, counts[mode]
        arrive(group, take, phase)
        take[group.mine] = send[group.mine]
        total = [jnp.zeros((share, rank), F32) for _ in range(count)]
        for u in range(group.size):
            rows = take[u, 0:share, :]
            for g in range(count):
                total[g] = total[g] + rows * take[u, share + g : share + g + 1, :]
        return jnp.concatenate(total, axis=0)

    def line_copy(group, buffer, step, column):
        slot = buffer.at[p * n_j + column]
        return pltpu.make_async_remote_copy(
            src_ref=slot,
            dst_ref=slot,
            send_sem=line_sems.at[0, step],
            recv_sem=line_sems.at[1, step],
            device_id=(p, shifted[1][step], s),
            device_id_type=MESH,
        )

    def start_relay(group, buffer, phase):
        for step in range(1, n_j):
            line_copy(group, buffer, step, q).start()
        slot = buffer.at[group.mine]
        lines[0].partners(lambda other, device: copy(slot, slot, phase, device).start())

    def end_relay(group, buffer, phase):
        for step in range(1, n_j):
            column = shifted[1][n_j - step]
            line_copy(group, buffer, step, column).wait_recv()
            slot = buffer.at[p * n_j + column]
            lines[0].partners(
                lambda other, device, slot=slot: copy(slot, slot, phase, device).start()
            )
        copy(*[buffer.at[pl.ds(0, (n_i - 1) * n_j)]] * 2, phase, position).wait_recv()

    def settle(mode, send, take, shares, sums, out, phase, inverse_of, gram_away, relay=False):
        group = groups[mode]
        share = extents[mode] // group.size
        shares[group.mine] = gather_cut(mode, send, take, phase)
        if relay:
            start_relay(group, shares, phase + 2)
        else:
            spread(group, shares, phase + 2)
        inverse = inverse_of()
        if relay:
            end_relay(group, shares, phase + 2)
        else:
            arrive(group, shares, phase + 2)
        solved = dot_high(shares[...].reshape(spans[mode], rank), inverse)
        sums[lines[mode].mine] = jnp.sum(solved * solved, axis=0, keepdims=True)
        spread(lines[mode], sums, phase + 1)
        gram_away(solved)
        arrive(lines[mode], sums, phase + 1)
        scale = lax.rsqrt(jnp.sum(sums[...], axis=0) / lengths[mode] + EPSILON)
        scaled = solved * scale
        for u in range(group.size):
            for g in range(counts[mode]):
                start = g * extents[mode] + u * share
                source = (u * counts[mode] + g) * share
                out[start : start + share, :] = scaled[source : source + share, :]
        return scale

    def scaled_gram(gram, scale):
        return gram * jnp.broadcast_to(scale, (rank, rank)).T * scale

    def stand_up():
        depth = CHUNK * extents[1]
        for start in range(0, tensor.shape[0], depth):
            upright[:, start : start + depth] = tensor[start : start + depth, :].T

    turn_slices(plane_b, slices_b, whole_b, 0)
    rows = product(0, block_rows(1, factor_b), block_rows(2, factor_c))
    cut(0, rows, send_0, take_0, 3)
    stand_up()
    first = {}

    def inverse_0():
        arrive(lines[2], gram_c_buf, 2)
        first["c"] = jnp.sum(gram_c_buf[...], axis=0) / lengths[2]
        return system_inverse(end_slices(whole_b, 0), first["c"])

    def gram_away_0(solved):
        plane_a_buf[p] = gram_of(solved)
        spread(lines[0], plane_a_buf, 6)

    scale_a = settle(0, send_0, take_0, share_0, sums_0, out_a, 3, inverse_0, gram_away_0)
    gram_c = first["c"]

    rows = product(1, block_rows(0, out_a), block_rows(2, factor_c))
    cut(1, rows, send_1, take_1, 7)

    def inverse_1():
        arrive(lines[0], plane_a_buf, 6)
        total = jnp.sum(plane_a_buf[...], axis=0) / lengths[0]
        first["a"] = scaled_gram(total, scale_a)
        return system_inverse(first["a"], gram_c)

    def gram_away_1(solved):
        start_slices(gram_of(solved), plane_2, slices_2, 10)

    scale_b = settle(1, send_1, take_1, share_1, sums_1, out_b, 7, inverse_1, gram_away_1)
    gram_a = first["a"]

    rows = product(2, block_rows(0, out_a), block_rows(1, out_b))
    cut(2, rows, send_2, take_2, 12)
    turn_slices(plane_2, slices_2, whole_2, 10)

    def inverse_2():
        return system_inverse(gram_a, scaled_gram(end_slices(whole_2, 10), scale_b))

    settle(
        2, send_2, take_2, share_2, sums_2, out_c, 12, inverse_2, lambda solved: None, relay=True
    )

    sent(lines[1], slices_b, 0)
    sent(groups[1], whole_b, 1)
    sent(lines[2], gram_c_buf, 2)
    sent(groups[0], send_0, 3)
    sent(lines[0], sums_0, 4)
    sent(groups[0], share_0, 5)
    sent(lines[0], plane_a_buf, 6)
    sent(groups[1], send_1, 7)
    sent(lines[1], sums_1, 8)
    sent(groups[1], share_1, 9)
    sent(lines[1], slices_2, 10)
    sent(groups[1], whole_2, 11)
    sent(groups[2], send_2, 12)
    sent(lines[2], sums_2, 13)
    for step in range(1, n_j):
        line_copy(groups[2], share_2, step, q).wait_send()
    copy(*[share_2.at[pl.ds(0, (n_i - 1) * n_j)]] * 2, 14, position).wait_send()


def store_kernel(one, two, three, out_one, out_two, out_three, sems):
    copies = [
        pltpu.make_async_copy(source, target, sems.at[i])
        for i, (source, target) in enumerate(((one, out_one), (two, out_two), (three, out_three)))
    ]
    for copy in copies:
        copy.start()
    for copy in copies:
        copy.wait()


def on_device(sizes, blocks, coords, live, factor_b, factor_c):
    n_i, n_j, n_k = sizes
    n_all = n_i * n_j * n_k
    slots, bi, bj, bk = blocks.shape
    rank = factor_b.shape[1]
    group_sizes = (n_j * n_k, n_i * n_k, n_i * n_j)
    spans = (GI_DEV * bi, factor_b.shape[0], factor_c.shape[0])
    extents = (bi, bj, bk)

    def message(mode):
        rows = extents[mode] // group_sizes[mode] + spans[mode] // extents[mode]
        return (group_sizes[mode], (rows + 7) // 8 * 8, rank)

    def buffer(*shape):
        return pltpu.VMEM(shape, F32)

    slices = [
        buffer(group_sizes[1], rank // group_sizes[1], rank),
        buffer(n_j, rank // group_sizes[1], rank),
        buffer(group_sizes[1], rank // group_sizes[1], rank),
    ]
    vmem = pl.BlockSpec(memory_space=pltpu.VMEM)
    far = pl.BlockSpec(memory_space=pltpu.HBM)
    shapes = [jax.ShapeDtypeStruct((span, rank), F32) for span in spans]
    factors = pl.pallas_call(
        functools.partial(kernel, sizes),
        out_shape=shapes,
        in_specs=[pl.BlockSpec(memory_space=pltpu.SMEM), far, far, far],
        out_specs=[vmem] * 3,
        scratch_shapes=[
            pltpu.VMEM((bi * bj, bk), BF16),
            buffer(*factor_b.shape),
            buffer(*factor_c.shape),
            buffer(bi * bj, bk),
            pltpu.VMEM((bj, bi, bk), BF16),
            pltpu.VMEM((bk, bi * bj), BF16),
            buffer(max(bi, bj), rank),
            *slices,
            buffer(n_k, rank, rank),
            buffer(n_i, rank, rank),
            *slices,
            *[buffer(*message(mode)) for mode in range(3)],
            *[buffer(*message(mode)) for mode in range(3)],
            *[buffer(group_sizes[mode], spans[mode] // group_sizes[mode], rank) for mode in range(3)],
            *[buffer(size, 1, rank) for size in sizes],
            pltpu.SemaphoreType.DMA((3,)),
            pltpu.SemaphoreType.DMA((2, 15)),
            pltpu.SemaphoreType.DMA((2, n_j)),
        ],
        compiler_params=pltpu.CompilerParams(
            collective_id=0, has_side_effects=True, vmem_limit_bytes=48 * 1024 * 1024
        ),
    )(
        coords.reshape(coords.shape[0]),
        *(
            pltpu.with_memory_space_constraint(array, pltpu.HBM)
            for array in (blocks.reshape(slots * bi * bj, bk), factor_b, factor_c)
        ),
    )
    return pl.pallas_call(
        store_kernel,
        out_shape=[jax.ShapeDtypeStruct((span, rank), F32) for span in spans],
        in_specs=[vmem] * 3,
        out_specs=[far] * 3,
        scratch_shapes=[pltpu.SemaphoreType.DMA((3,))],
    )(*factors)


def solution(mesh):
    sizes = (mesh.shape["ia"], mesh.shape["ja"], mesh.shape["ka"])
    placed = (
        P(("ia", "ja", "ka"), None, None, None),
        P(None, ("ia", "ja", "ka")),
        P(("ia", "ja", "ka")),
        P("ja", None),
        P("ka", None),
    )
    return jax.shard_map(
        functools.partial(on_device, sizes),
        mesh=mesh,
        in_specs=placed,
        out_specs=(P("ia", None), P("ja", None), P("ka", None)),
        check_vma=False,
    )
```

```python
import functools

import jax
import jax.numpy as jnp
from jax import lax
from jax.experimental import pallas as pl
from jax.experimental.pallas import tpu as pltpu
from jax.sharding import PartitionSpec as P

GI_DEV = 4
RIDGE_SHARE = 0.3
EPSILON = 1e-06
HIGHEST = lax.Precision.HIGHEST
MESH = pl.DeviceIdType.MESH
F32 = jnp.float32
BF16 = jnp.bfloat16
CHUNK = 8


def newton_plan(order):
    low = RIDGE_SHARE / order
    high = 1.0 + low
    first = 2.0 / (low + high)
    error = (high - low) / (high + low)
    scales = []
    while error > 1e-9:
        square = error * error
        scales.append(2.0 / (2.0 - square))
        error = square / (2.0 - square)
    return first, scales


def dot_high(left, right):
    return jnp.dot(left, right, precision=HIGHEST, preferred_element_type=F32)


def halves(values):
    head = values.astype(BF16)
    return head, (values - head.astype(F32)).astype(BF16)


def dot_middle(left, right):
    left_head, left_tail = halves(left)
    right_head, right_tail = halves(right)

    def times(one, two):
        return jnp.dot(one, two, preferred_element_type=F32)

    return times(left_head, right_head) + (
        times(left_head, right_tail) + times(left_tail, right_head)
    )


def system_inverse(gram_one, gram_two):
    order = gram_one.shape[0]
    merged = gram_one * gram_two
    on_diagonal = lax.broadcasted_iota(jnp.int32, (order, order), 0) == lax.broadcasted_iota(
        jnp.int32, (order, order), 1
    )
    eye = jnp.where(on_diagonal, 1.0, 0.0).astype(F32)
    trace = jnp.sum(jnp.sum(merged * eye, axis=1, keepdims=True), axis=0, keepdims=True)
    unit = 1.0 / trace
    system = merged * unit + (RIDGE_SHARE / order) * eye
    first, scales = newton_plan(order)
    twice = 2.0 * eye
    start = scales[0] * first
    guess = start * (twice - first * system)
    image = start * (2.0 * system - first * dot_middle(system, system))
    for scale in scales[1:-1]:
        both = scale * dot_middle(jnp.concatenate([image, guess], axis=0), twice - image)
        image, guess = both[:order], both[order:]
    guess = scales[-1] * dot_high(guess, twice - dot_high(system, guess))
    return guess * unit


def gram_of(values):
    return lax.dot_general(
        values, values, (((0,), (0,)), ((), ())), precision=HIGHEST, preferred_element_type=F32
    )


def kernel(
    sizes,
    coords,
    tensor_hbm,
    factor_b_hbm,
    factor_c_hbm,
    out_a,
    out_b,
    out_c,
    tensor,
    factor_b,
    factor_c,
    wide,
    turned,
    upright,
    rows_one,
    plane_b,
    slices_b,
    whole_b,
    gram_c_buf,
    plane_a_buf,
    plane_2,
    slices_2,
    whole_2,
    send_0,
    send_2,
    take_0,
    take_2,
    share_0,
    all_1,
    share_2,
    own_sums,
    sums_0,
    sums_1,
    sums_2,
    load_sems,
    sems,
    line_sems,
):
    n_i, n_j, n_k = sizes
    n_all = n_i * n_j * n_k
    p, q, s = lax.axis_index("ia"), lax.axis_index("ja"), lax.axis_index("ka")
    spans = (out_a.shape[0], out_b.shape[0], out_c.shape[0])
    extents = (turned.shape[1], turned.shape[0], turned.shape[2])
    counts = tuple(span // extent for span, extent in zip(spans, extents))
    lengths = (spans[0] * n_i, spans[1] * n_j, spans[2] * n_k)
    rank = out_a.shape[1]

    loads = [
        pltpu.make_async_copy(source, target, load_sems.at[i])
        for i, (source, target) in enumerate(
            ((factor_b_hbm, factor_b), (factor_c_hbm, factor_c), (tensor_hbm, tensor))
        )
    ]
    for load in loads:
        load.start()

    position = (p, q, s)
    shifted = [
        [lax.rem(place + offset, size) for offset in range(size)]
        for place, size in zip(position, sizes)
    ]

    class Group:
        def __init__(self, *axes):
            self.axes = axes
            self.size = 1
            self.mine = 0
            for axis in axes:
                self.size *= sizes[axis]
                self.mine = self.mine * sizes[axis] + position[axis]

        def outside(self, body):
            (axis,) = (i for i in range(3) if i not in self.axes)

            def visit(step, index):
                device, rest, slot = list(position), index, (step - 1) * self.size + self.mine
                device[axis] = lax.rem(position[axis] + step, sizes[axis])
                for other in reversed(self.axes):
                    if isinstance(rest, int):
                        device[other] = shifted[other][rest % sizes[other]]
                    else:
                        device[other] = lax.rem(rest, sizes[other])
                    rest = rest // sizes[other]
                body(slot, tuple(device))

            for step in range(1, sizes[axis]):
                if self.size <= 16:
                    for index in range(self.size):
                        visit(step, index)
                else:
                    pl.loop(0, self.size)(functools.partial(visit, step))

        def partners(self, body):
            if self.size <= 32:
                for offset in range(1, self.size):
                    device, other, rest = list(position), 0, []
                    for axis in reversed(self.axes):
                        rest.append(offset % sizes[axis])
                        offset //= sizes[axis]
                    for axis, step in zip(self.axes, reversed(rest)):
                        device[axis] = shifted[axis][step]
                        other = other * sizes[axis] + device[axis]
                    body(other, tuple(device))
            else:

                @pl.loop(1, self.size)
                def _(offset):
                    other = lax.rem(self.mine + offset, self.size)
                    device, rest = list(position), other
                    for axis in reversed(self.axes):
                        device[axis] = lax.rem(rest, sizes[axis])
                        rest = rest // sizes[axis]
                    body(other, tuple(device))

    everyone = Group(0, 1, 2)
    groups = (Group(1, 2), Group(0, 2), Group(0, 1))
    lines = (Group(0), Group(1), Group(2))

    def copy(source, target, phase, device):
        return pltpu.make_async_remote_copy(
            src_ref=source,
            dst_ref=target,
            send_sem=sems.at[0, phase],
            recv_sem=sems.at[1, phase],
            device_id=device,
            device_id_type=MESH,
        )

    def all_but_one(group, buffer, phase):
        part = buffer.at[pl.ds(0, group.size - 1)]
        return copy(part, part, phase, tuple(row[-1] for row in shifted))

    def spread(group, buffer, phase):
        slot = buffer.at[group.mine]
        group.partners(lambda other, device: copy(slot, slot, phase, device).start())

    def deal(group, source, target, phase):
        group.partners(
            lambda other, device: copy(
                source.at[other], target.at[group.mine], phase, device
            ).start()
        )

    def arrive(group, buffer, phase):
        all_but_one(group, buffer, phase).wait_recv()

    def sent(group, buffer, phase):
        all_but_one(group, buffer, phase).wait_send()

    barrier = pltpu.get_barrier_semaphore()
    everyone.partners(
        lambda other, device: pl.semaphore_signal(
            barrier, inc=1, device_id=device, device_id_type=MESH
        )
    )

    def store_slices(gram, plane):
        share = plane.shape[1]
        for u in range(plane.shape[0]):
            plane[u] = gram[u * share : (u + 1) * share, :]

    def start_slices(gram, plane, slices, phase):
        store_slices(gram, plane)
        mine = plane.at[groups[1].mine]
        target = slices.at[q]
        lines[1].partners(lambda other, device: copy(mine, target, phase, device).start())

    def turn_slices(plane, slices, whole, phase):
        arrive(lines[1], slices, phase)
        slices[q] = plane[groups[1].mine]
        whole[groups[1].mine] = jnp.sum(slices[...], axis=0)
        spread(groups[1], whole, phase + 1)

    def end_slices(whole, phase):
        arrive(groups[1], whole, phase + 1)
        return whole[...].reshape(rank, rank) / lengths[1]

    loads[0].wait()
    first_gram_b = gram_of(factor_b[...])
    loads[1].wait()
    gram_c_buf[s] = gram_of(factor_c[...])
    pl.semaphore_wait(barrier, n_all - 1)
    start_slices(first_gram_b, plane_b, slices_b, 0)
    spread(lines[2], gram_c_buf, 2)

    def marks_of(mode, base):
        row = lax.broadcasted_iota(jnp.int32, (counts[mode], rank), 0) + base
        return jnp.where(row == jnp.full(row.shape, coords[mode], jnp.int32), 1.0, 0.0)

    marks = (marks_of(0, p * counts[0]), marks_of(1, q * counts[1]), marks_of(2, s * counts[2]))

    def block_rows(mode, source):
        extent = extents[mode]
        return sum(
            source[g * extent : (g + 1) * extent, :] * marks[mode][g : g + 1, :]
            for g in range(counts[mode])
        )

    loads[2].wait()
    wide[...] = tensor[...].astype(F32)

    @pl.loop(0, extents[1], unroll=8)
    def _(b):
        turned[b] = wide[pl.ds(b, extents[0], stride=extents[1]), :].astype(BF16)

    def product(mode, rows_of_one, rows_of_two):
        rows_one[0 : rows_of_one.shape[0], :] = rows_of_one
        total = jnp.zeros((extents[mode], rank), F32)

        def step(j, total):
            ones = rows_one[pl.ds(pl.multiple_of(j * CHUNK, CHUNK), CHUNK), :]
            khatri = jnp.concatenate(
                [(ones[i : i + 1, :] * rows_of_two).astype(BF16) for i in range(CHUNK)], axis=0
            )
            if mode == 2:
                depth = CHUNK * extents[1]
                left = upright[:, pl.ds(pl.multiple_of(j * depth, depth), depth)]
            else:
                if mode == 0:
                    parts = [turned[j * CHUNK + i] for i in range(CHUNK)]
                else:
                    height = extents[1]
                    parts = [
                        tensor[pl.ds(pl.multiple_of((j * CHUNK + i) * height, height), height), :]
                        for i in range(CHUNK)
                    ]
                left = jnp.concatenate(parts, axis=1)
            return total + jnp.dot(left, khatri, preferred_element_type=F32)

        return lax.fori_loop(0, rows_of_one.shape[0] // CHUNK, step, total, unroll=True)

    def cut(mode, rows, send, take, phase):
        group = groups[mode]
        share = extents[mode] // group.size
        for u in range(group.size):
            send[u, 0:share, :] = rows[u * share : (u + 1) * share, :]
            send[u, share : share + counts[mode], :] = marks[mode]
        deal(group, send, take, phase)

    def gather_cut(mode, send, take, phase):
        group = groups[mode]
        share, count = extents[mode] // group.size, counts[mode]
        arrive(group, take, phase)
        take[group.mine] = send[group.mine]
        total = [jnp.zeros((share, rank), F32) for _ in range(count)]
        for u in range(group.size):
            rows = take[u, 0:share, :]
            for g in range(count):
                total[g] = total[g] + rows * take[u, share + g : share + g + 1, :]
        return jnp.concatenate(total, axis=0)

    def line_copy(group, buffer, step, column):
        slot = buffer.at[p * n_j + column]
        return pltpu.make_async_remote_copy(
            src_ref=slot,
            dst_ref=slot,
            send_sem=line_sems.at[0, step],
            recv_sem=line_sems.at[1, step],
            device_id=(p, shifted[1][step], s),
            device_id_type=MESH,
        )

    def start_relay(group, buffer, phase):
        for step in range(1, n_j):
            line_copy(group, buffer, step, q).start()
        slot = buffer.at[group.mine]
        lines[0].partners(lambda other, device: copy(slot, slot, phase, device).start())

    def end_relay(group, buffer, phase):
        for step in range(1, n_j):
            column = shifted[1][n_j - step]
            line_copy(group, buffer, step, column).wait_recv()
            slot = buffer.at[p * n_j + column]
            lines[0].partners(
                lambda other, device, slot=slot: copy(slot, slot, phase, device).start()
            )
        copy(*[buffer.at[pl.ds(0, (n_i - 1) * n_j)]] * 2, phase, position).wait_recv()

    def settle(mode, send, take, inverse, shares, sums, out, phase, meanwhile=None, relay=False):
        group = groups[mode]
        share = extents[mode] // group.size
        solved = dot_high(gather_cut(mode, send, take, phase), inverse)
        shares[group.mine] = solved
        if relay:
            start_relay(group, shares, phase + 2)
        else:
            spread(group, shares, phase + 2)
        own_sums[mode] = jnp.sum(solved * solved, axis=0, keepdims=True)
        group.outside(
            lambda slot, device: copy(
                own_sums.at[mode], sums.at[slot], phase + 1, device
            ).start()
        )
        if meanwhile is not None:
            meanwhile()
        if relay:
            end_relay(group, shares, phase + 2)
        else:
            arrive(group, shares, phase + 2)
        copy(sums, sums, phase + 1, position).wait_recv()
        squares = jnp.sum(sums[...], axis=0)
        for u in range(group.size):
            squares = squares + jnp.sum(shares[u] * shares[u], axis=0, keepdims=True)
        squares = squares / lengths[mode]
        scale = lax.rsqrt(squares + EPSILON)
        for u in range(group.size):
            rows = shares[u] * scale
            for g in range(counts[mode]):
                start = g * extents[mode] + u * share
                out[start : start + share, :] = rows[g * share : (g + 1) * share, :]

    def stand_up():
        depth = CHUNK * extents[1]
        for start in range(0, tensor.shape[0], depth):
            upright[:, start : start + depth] = tensor[start : start + depth, :].T

    def scaled_gram(gram, scale):
        return gram * jnp.broadcast_to(scale, (rank, rank)).T * scale

    turn_slices(plane_b, slices_b, whole_b, 0)
    rows = product(0, block_rows(1, factor_b), block_rows(2, factor_c))
    cut(0, rows, send_0, take_0, 3)
    arrive(lines[2], gram_c_buf, 2)
    gram_c = jnp.sum(gram_c_buf[...], axis=0) / lengths[2]
    gram_b = end_slices(whole_b, 0)
    inverse = system_inverse(gram_b, gram_c)
    settle(0, send_0, take_0, inverse, share_0, sums_0, out_a, 3, stand_up)
    plane_a_buf[p] = gram_of(out_a[...])
    spread(lines[0], plane_a_buf, 6)

    rows = product(1, block_rows(0, out_a), block_rows(2, factor_c))
    height, mine = extents[1], groups[1].mine
    all_1[mine, 0:height, :] = rows
    all_1[mine, height : height + counts[1], :] = marks[1]
    spread(groups[1], all_1, 7)
    arrive(lines[0], plane_a_buf, 6)
    gram_a = jnp.sum(plane_a_buf[...], axis=0) / lengths[0]
    inverse = system_inverse(gram_a, gram_c)
    arrive(groups[1], all_1, 7)
    summed = jnp.concatenate(
        [
            sum(
                all_1[u, 0:height, :] * all_1[u, height + g : height + g + 1, :]
                for u in range(groups[1].size)
            )
            for g in range(counts[1])
        ],
        axis=0,
    )
    solved = dot_high(summed, inverse)
    sums_1[q] = jnp.sum(solved * solved, axis=0, keepdims=True)
    spread(lines[1], sums_1, 8)
    start_slices(gram_of(solved), plane_2, slices_2, 10)
    arrive(lines[1], sums_1, 8)
    scale_b = lax.rsqrt(jnp.sum(sums_1[...], axis=0) / lengths[1] + EPSILON)
    out_b[...] = solved * scale_b

    turn_slices(plane_2, slices_2, whole_2, 10)
    rows = product(2, block_rows(0, out_a), block_rows(1, out_b))
    cut(2, rows, send_2, take_2, 12)
    gram_b = scaled_gram(end_slices(whole_2, 10), scale_b)
    inverse = system_inverse(gram_a, gram_b)
    settle(2, send_2, take_2, inverse, share_2, sums_2, out_c, 12, relay=True)

    sent(lines[1], slices_b, 0)
    sent(groups[1], whole_b, 1)
    sent(lines[2], gram_c_buf, 2)
    sent(groups[0], send_0, 3)
    copy(sums_0, sums_0, 4, position).wait_send()
    sent(groups[0], share_0, 5)
    sent(lines[0], plane_a_buf, 6)
    sent(groups[1], all_1, 7)
    sent(lines[1], sums_1, 8)
    sent(lines[1], slices_2, 10)
    sent(groups[1], whole_2, 11)
    sent(groups[2], send_2, 12)
    copy(sums_2, sums_2, 13, position).wait_send()
    for step in range(1, n_j):
        line_copy(groups[2], share_2, step, q).wait_send()
    copy(*[share_2.at[pl.ds(0, (n_i - 1) * n_j)]] * 2, 14, position).wait_send()


def on_device(sizes, blocks, coords, live, factor_b, factor_c):
    n_i, n_j, n_k = sizes
    n_all = n_i * n_j * n_k
    slots, bi, bj, bk = blocks.shape
    rank = factor_b.shape[1]
    group_sizes = (n_j * n_k, n_i * n_k, n_i * n_j)
    spans = (GI_DEV * bi, factor_b.shape[0], factor_c.shape[0])
    extents = (bi, bj, bk)

    def message(mode):
        rows = extents[mode] // group_sizes[mode] + spans[mode] // extents[mode]
        return (group_sizes[mode], (rows + 7) // 8 * 8, rank)

    def buffer(*shape):
        return pltpu.VMEM(shape, F32)

    slices = [
        buffer(group_sizes[1], rank // group_sizes[1], rank),
        buffer(n_j, rank // group_sizes[1], rank),
        buffer(group_sizes[1], rank // group_sizes[1], rank),
    ]
    vmem = pl.BlockSpec(memory_space=pltpu.VMEM)
    far = pl.BlockSpec(memory_space=pltpu.HBM)
    shapes = [jax.ShapeDtypeStruct((span, rank), F32) for span in spans]
    return pl.pallas_call(
        functools.partial(kernel, sizes),
        out_shape=shapes,
        in_specs=[pl.BlockSpec(memory_space=pltpu.SMEM), far, far, far],
        out_specs=[vmem] * 3,
        scratch_shapes=[
            pltpu.VMEM((bi * bj, bk), BF16),
            buffer(*factor_b.shape),
            buffer(*factor_c.shape),
            buffer(bi * bj, bk),
            pltpu.VMEM((bj, bi, bk), BF16),
            pltpu.VMEM((bk, bi * bj), BF16),
            buffer(max(bi, bj), rank),
            *slices,
            buffer(n_k, rank, rank),
            buffer(n_i, rank, rank),
            *slices,
            *[buffer(*message(mode)) for mode in (0, 2)],
            *[buffer(*message(mode)) for mode in (0, 2)],
            buffer(group_sizes[0], spans[0] // group_sizes[0], rank),
            buffer(group_sizes[1], bj + (spans[1] // bj + 7) // 8 * 8, rank),
            buffer(group_sizes[2], spans[2] // group_sizes[2], rank),
            buffer(3, 1, rank),
            buffer(n_all - group_sizes[0], 1, rank),
            buffer(n_j, 1, rank),
            buffer(n_all - group_sizes[2], 1, rank),
            pltpu.SemaphoreType.DMA((3,)),
            pltpu.SemaphoreType.DMA((2, 15)),
            pltpu.SemaphoreType.DMA((2, n_j)),
        ],
        compiler_params=pltpu.CompilerParams(
            collective_id=0, has_side_effects=True, vmem_limit_bytes=48 * 1024 * 1024
        ),
    )(
        coords.reshape(coords.shape[0]),
        *(
            pltpu.with_memory_space_constraint(array, pltpu.HBM)
            for array in (blocks.reshape(slots * bi * bj, bk), factor_b, factor_c)
        ),
    )


def solution(mesh):
    sizes = (mesh.shape["ia"], mesh.shape["ja"], mesh.shape["ka"])
    placed = (
        P(("ia", "ja", "ka"), None, None, None),
        P(None, ("ia", "ja", "ka")),
        P(("ia", "ja", "ka")),
        P("ja", None),
        P("ka", None),
    )
    return jax.shard_map(
        functools.partial(on_device, sizes),
        mesh=mesh,
        in_specs=placed,
        out_specs=(P("ia", None), P("ja", None), P("ka", None)),
        check_vma=False,
    )
```

```python
import functools

import jax
import jax.numpy as jnp
from jax import lax
from jax.experimental import pallas as pl
from jax.experimental.pallas import tpu as pltpu
from jax.sharding import PartitionSpec as P

GI_DEV = 4
RIDGE_SHARE = 0.3
EPSILON = 1e-06
HIGHEST = lax.Precision.HIGHEST
MESH = pl.DeviceIdType.MESH
F32 = jnp.float32
BF16 = jnp.bfloat16
CHUNK = 8


def newton_plan(order):
    low = RIDGE_SHARE / order
    high = 1.0 + low
    first = 2.0 / (low + high)
    error = (high - low) / (high + low)
    scales = []
    while error > 1e-9:
        square = error * error
        scales.append(2.0 / (2.0 - square))
        error = square / (2.0 - square)
    return first, scales


def dot_high(left, right):
    return jnp.dot(left, right, precision=HIGHEST, preferred_element_type=F32)


def halves(values):
    head = values.astype(BF16)
    return head, (values - head.astype(F32)).astype(BF16)


def dot_middle(left, right):
    left_head, left_tail = halves(left)
    right_head, right_tail = halves(right)

    def times(one, two):
        return jnp.dot(one, two, preferred_element_type=F32)

    return times(left_head, right_head) + (
        times(left_head, right_tail) + times(left_tail, right_head)
    )


def system_inverse(gram_one, gram_two):
    order = gram_one.shape[0]
    merged = gram_one * gram_two
    on_diagonal = lax.broadcasted_iota(jnp.int32, (order, order), 0) == lax.broadcasted_iota(
        jnp.int32, (order, order), 1
    )
    eye = jnp.where(on_diagonal, 1.0, 0.0).astype(F32)
    trace = jnp.sum(jnp.sum(merged * eye, axis=1, keepdims=True), axis=0, keepdims=True)
    unit = 1.0 / trace
    system = merged * unit + (RIDGE_SHARE / order) * eye
    first, scales = newton_plan(order)
    twice = 2.0 * eye
    start = scales[0] * first
    guess = start * (twice - first * system)
    image = start * (2.0 * system - first * dot_middle(system, system))
    for scale in scales[1:-1]:
        both = scale * dot_middle(jnp.concatenate([image, guess], axis=0), twice - image)
        image, guess = both[:order], both[order:]
    guess = scales[-1] * dot_high(guess, twice - dot_high(system, guess))
    return guess * unit


def gram_of(values):
    return lax.dot_general(
        values, values, (((0,), (0,)), ((), ())), precision=HIGHEST, preferred_element_type=F32
    )


def kernel(
    sizes,
    coords_hbm,
    tensor_hbm,
    factor_b_hbm,
    factor_c_hbm,
    out_a,
    out_b,
    out_c,
    coords,
    tensor,
    factor_b,
    factor_c,
    wide,
    turned,
    upright,
    rows_one,
    plane_b,
    slices_b,
    whole_b,
    gram_c_buf,
    plane_a_buf,
    plane_2,
    slices_2,
    whole_2,
    send_0,
    send_2,
    take_0,
    take_2,
    share_0,
    all_1,
    share_2,
    own_sums,
    sums_0,
    sums_1,
    sums_2,
    load_sems,
    sems,
    line_sems,
):
    n_i, n_j, n_k = sizes
    n_all = n_i * n_j * n_k
    p, q, s = lax.axis_index("ia"), lax.axis_index("ja"), lax.axis_index("ka")
    spans = (out_a.shape[0], out_b.shape[0], out_c.shape[0])
    extents = (turned.shape[1], turned.shape[0], turned.shape[2])
    counts = tuple(span // extent for span, extent in zip(spans, extents))
    lengths = (spans[0] * n_i, spans[1] * n_j, spans[2] * n_k)
    rank = out_a.shape[1]

    loads = [
        pltpu.make_async_copy(source, target, load_sems.at[i])
        for i, (source, target) in enumerate(
            ((factor_b_hbm, factor_b), (factor_c_hbm, factor_c), (tensor_hbm, tensor), (coords_hbm, coords))
        )
    ]
    for load in loads:
        load.start()

    position = (p, q, s)
    shifted = [
        [lax.rem(place + offset, size) for offset in range(size)]
        for place, size in zip(position, sizes)
    ]

    class Group:
        def __init__(self, *axes):
            self.axes = axes
            self.size = 1
            self.mine = 0
            for axis in axes:
                self.size *= sizes[axis]
                self.mine = self.mine * sizes[axis] + position[axis]

        def outside(self, body):
            (axis,) = (i for i in range(3) if i not in self.axes)

            def visit(step, index):
                device, rest, slot = list(position), index, (step - 1) * self.size + self.mine
                device[axis] = lax.rem(position[axis] + step, sizes[axis])
                for other in reversed(self.axes):
                    if isinstance(rest, int):
                        device[other] = shifted[other][rest % sizes[other]]
                    else:
                        device[other] = lax.rem(rest, sizes[other])
                    rest = rest // sizes[other]
                body(slot, tuple(device))

            for step in range(1, sizes[axis]):
                if self.size <= 16:
                    for index in range(self.size):
                        visit(step, index)
                else:
                    pl.loop(0, self.size)(functools.partial(visit, step))

        def partners(self, body):
            if self.size <= 32:
                for offset in range(1, self.size):
                    device, other, rest = list(position), 0, []
                    for axis in reversed(self.axes):
                        rest.append(offset % sizes[axis])
                        offset //= sizes[axis]
                    for axis, step in zip(self.axes, reversed(rest)):
                        device[axis] = shifted[axis][step]
                        other = other * sizes[axis] + device[axis]
                    body(other, tuple(device))
            else:

                @pl.loop(1, self.size)
                def _(offset):
                    other = lax.rem(self.mine + offset, self.size)
                    device, rest = list(position), other
                    for axis in reversed(self.axes):
                        device[axis] = lax.rem(rest, sizes[axis])
                        rest = rest // sizes[axis]
                    body(other, tuple(device))

    everyone = Group(0, 1, 2)
    groups = (Group(1, 2), Group(0, 2), Group(0, 1))
    lines = (Group(0), Group(1), Group(2))

    def copy(source, target, phase, device):
        return pltpu.make_async_remote_copy(
            src_ref=source,
            dst_ref=target,
            send_sem=sems.at[0, phase],
            recv_sem=sems.at[1, phase],
            device_id=device,
            device_id_type=MESH,
        )

    def all_but_one(group, buffer, phase):
        part = buffer.at[pl.ds(0, group.size - 1)]
        return copy(part, part, phase, tuple(row[-1] for row in shifted))

    def spread(group, buffer, phase):
        slot = buffer.at[group.mine]
        group.partners(lambda other, device: copy(slot, slot, phase, device).start())

    def deal(group, source, target, phase):
        group.partners(
            lambda other, device: copy(
                source.at[other], target.at[group.mine], phase, device
            ).start()
        )

    def arrive(group, buffer, phase):
        all_but_one(group, buffer, phase).wait_recv()

    def sent(group, buffer, phase):
        all_but_one(group, buffer, phase).wait_send()

    barrier = pltpu.get_barrier_semaphore()
    everyone.partners(
        lambda other, device: pl.semaphore_signal(
            barrier, inc=1, device_id=device, device_id_type=MESH
        )
    )

    def store_slices(gram, plane):
        share = plane.shape[1]
        for u in range(plane.shape[0]):
            plane[u] = gram[u * share : (u + 1) * share, :]

    def start_slices(gram, plane, slices, phase):
        store_slices(gram, plane)
        mine = plane.at[groups[1].mine]
        target = slices.at[q]
        lines[1].partners(lambda other, device: copy(mine, target, phase, device).start())

    def turn_slices(plane, slices, whole, phase):
        arrive(lines[1], slices, phase)
        slices[q] = plane[groups[1].mine]
        whole[groups[1].mine] = jnp.sum(slices[...], axis=0)
        spread(groups[1], whole, phase + 1)

    def end_slices(whole, phase):
        arrive(groups[1], whole, phase + 1)
        return whole[...].reshape(rank, rank) / lengths[1]

    loads[0].wait()
    first_gram_b = gram_of(factor_b[...])
    loads[1].wait()
    gram_c_buf[s] = gram_of(factor_c[...])
    loads[2].wait()
    wide[...] = tensor[...].astype(F32)
    loads[3].wait()
    pl.semaphore_wait(barrier, n_all - 1)
    start_slices(first_gram_b, plane_b, slices_b, 0)
    spread(lines[2], gram_c_buf, 2)

    def marks_of(mode, base):
        row = lax.broadcasted_iota(jnp.int32, (counts[mode], rank), 0) + base
        return jnp.where(row == jnp.full(row.shape, coords[mode], jnp.int32), 1.0, 0.0)

    marks = (marks_of(0, p * counts[0]), marks_of(1, q * counts[1]), marks_of(2, s * counts[2]))

    def block_rows(mode, source):
        extent = extents[mode]
        return sum(
            source[g * extent : (g + 1) * extent, :] * marks[mode][g : g + 1, :]
            for g in range(counts[mode])
        )

    @pl.loop(0, extents[1], unroll=8)
    def _(b):
        turned[b] = wide[pl.ds(b, extents[0], stride=extents[1]), :].astype(BF16)

    def product(mode, rows_of_one, rows_of_two):
        rows_one[0 : rows_of_one.shape[0], :] = rows_of_one
        total = jnp.zeros((extents[mode], rank), F32)

        def step(j, total):
            ones = rows_one[pl.ds(pl.multiple_of(j * CHUNK, CHUNK), CHUNK), :]
            khatri = jnp.concatenate(
                [(ones[i : i + 1, :] * rows_of_two).astype(BF16) for i in range(CHUNK)], axis=0
            )
            if mode == 2:
                depth = CHUNK * extents[1]
                left = upright[:, pl.ds(pl.multiple_of(j * depth, depth), depth)]
            else:
                if mode == 0:
                    parts = [turned[j * CHUNK + i] for i in range(CHUNK)]
                else:
                    height = extents[1]
                    parts = [
                        tensor[pl.ds(pl.multiple_of((j * CHUNK + i) * height, height), height), :]
                        for i in range(CHUNK)
                    ]
                left = jnp.concatenate(parts, axis=1)
            return total + jnp.dot(left, khatri, preferred_element_type=F32)

        return lax.fori_loop(0, rows_of_one.shape[0] // CHUNK, step, total, unroll=True)

    def cut(mode, rows, send, take, phase):
        group = groups[mode]
        share = extents[mode] // group.size
        for u in range(group.size):
            send[u, 0:share, :] = rows[u * share : (u + 1) * share, :]
            send[u, share : share + counts[mode], :] = marks[mode]
        deal(group, send, take, phase)

    def gather_cut(mode, send, take, phase):
        group = groups[mode]
        share, count = extents[mode] // group.size, counts[mode]
        arrive(group, take, phase)
        take[group.mine] = send[group.mine]
        total = [jnp.zeros((share, rank), F32) for _ in range(count)]
        for u in range(group.size):
            rows = take[u, 0:share, :]
            for g in range(count):
                total[g] = total[g] + rows * take[u, share + g : share + g + 1, :]
        return jnp.concatenate(total, axis=0)

    def line_copy(group, buffer, step, column):
        slot = buffer.at[p * n_j + column]
        return pltpu.make_async_remote_copy(
            src_ref=slot,
            dst_ref=slot,
            send_sem=line_sems.at[0, step],
            recv_sem=line_sems.at[1, step],
            device_id=(p, shifted[1][step], s),
            device_id_type=MESH,
        )

    def start_relay(group, buffer, phase):
        for step in range(1, n_j):
            line_copy(group, buffer, step, q).start()
        slot = buffer.at[group.mine]
        lines[0].partners(lambda other, device: copy(slot, slot, phase, device).start())

    def end_relay(group, buffer, phase):
        for step in range(1, n_j):
            column = shifted[1][n_j - step]
            line_copy(group, buffer, step, column).wait_recv()
            slot = buffer.at[p * n_j + column]
            lines[0].partners(
                lambda other, device, slot=slot: copy(slot, slot, phase, device).start()
            )
        copy(*[buffer.at[pl.ds(0, (n_i - 1) * n_j)]] * 2, phase, position).wait_recv()

    def settle(mode, send, take, inverse, shares, sums, out, phase, meanwhile=None, relay=False):
        group = groups[mode]
        share = extents[mode] // group.size
        solved = dot_high(gather_cut(mode, send, take, phase), inverse)
        shares[group.mine] = solved
        if relay:
            start_relay(group, shares, phase + 2)
        else:
            spread(group, shares, phase + 2)
        own_sums[mode] = jnp.sum(solved * solved, axis=0, keepdims=True)
        group.outside(
            lambda slot, device: copy(
                own_sums.at[mode], sums.at[slot], phase + 1, device
            ).start()
        )
        if meanwhile is not None:
            meanwhile()
        if relay:
            end_relay(group, shares, phase + 2)
        else:
            arrive(group, shares, phase + 2)
        copy(sums, sums, phase + 1, position).wait_recv()
        squares = jnp.sum(sums[...], axis=0)
        for u in range(group.size):
            squares = squares + jnp.sum(shares[u] * shares[u], axis=0, keepdims=True)
        squares = squares / lengths[mode]
        scale = lax.rsqrt(squares + EPSILON)
        for u in range(group.size):
            rows = shares[u] * scale
            for g in range(counts[mode]):
                start = g * extents[mode] + u * share
                out[start : start + share, :] = rows[g * share : (g + 1) * share, :]

    def stand_up():
        depth = CHUNK * extents[1]
        for start in range(0, tensor.shape[0], depth):
            upright[:, start : start + depth] = tensor[start : start + depth, :].T

    def scaled_gram(gram, scale):
        return gram * jnp.broadcast_to(scale, (rank, rank)).T * scale

    turn_slices(plane_b, slices_b, whole_b, 0)
    rows = product(0, block_rows(1, factor_b), block_rows(2, factor_c))
    cut(0, rows, send_0, take_0, 3)
    arrive(lines[2], gram_c_buf, 2)
    gram_c = jnp.sum(gram_c_buf[...], axis=0) / lengths[2]
    gram_b = end_slices(whole_b, 0)
    inverse = system_inverse(gram_b, gram_c)
    settle(0, send_0, take_0, inverse, share_0, sums_0, out_a, 3, stand_up)
    plane_a_buf[p] = gram_of(out_a[...])
    spread(lines[0], plane_a_buf, 6)

    rows = product(1, block_rows(0, out_a), block_rows(2, factor_c))
    height, mine = extents[1], groups[1].mine
    all_1[mine, 0:height, :] = rows
    all_1[mine, height : height + counts[1], :] = marks[1]
    spread(groups[1], all_1, 7)
    arrive(lines[0], plane_a_buf, 6)
    gram_a = jnp.sum(plane_a_buf[...], axis=0) / lengths[0]
    inverse = system_inverse(gram_a, gram_c)
    arrive(groups[1], all_1, 7)
    summed = jnp.concatenate(
        [
            sum(
                all_1[u, 0:height, :] * all_1[u, height + g : height + g + 1, :]
                for u in range(groups[1].size)
            )
            for g in range(counts[1])
        ],
        axis=0,
    )
    solved = dot_high(summed, inverse)
    sums_1[q] = jnp.sum(solved * solved, axis=0, keepdims=True)
    spread(lines[1], sums_1, 8)
    start_slices(gram_of(solved), plane_2, slices_2, 10)
    arrive(lines[1], sums_1, 8)
    scale_b = lax.rsqrt(jnp.sum(sums_1[...], axis=0) / lengths[1] + EPSILON)
    out_b[...] = solved * scale_b

    turn_slices(plane_2, slices_2, whole_2, 10)
    rows = product(2, block_rows(0, out_a), block_rows(1, out_b))
    cut(2, rows, send_2, take_2, 12)
    gram_b = scaled_gram(end_slices(whole_2, 10), scale_b)
    inverse = system_inverse(gram_a, gram_b)
    settle(2, send_2, take_2, inverse, share_2, sums_2, out_c, 12, relay=True)

    sent(lines[1], slices_b, 0)
    sent(groups[1], whole_b, 1)
    sent(lines[2], gram_c_buf, 2)
    sent(groups[0], send_0, 3)
    copy(sums_0, sums_0, 4, position).wait_send()
    sent(groups[0], share_0, 5)
    sent(lines[0], plane_a_buf, 6)
    sent(groups[1], all_1, 7)
    sent(lines[1], sums_1, 8)
    sent(lines[1], slices_2, 10)
    sent(groups[1], whole_2, 11)
    sent(groups[2], send_2, 12)
    copy(sums_2, sums_2, 13, position).wait_send()
    for step in range(1, n_j):
        line_copy(groups[2], share_2, step, q).wait_send()
    copy(*[share_2.at[pl.ds(0, (n_i - 1) * n_j)]] * 2, 14, position).wait_send()


def on_device(sizes, blocks, coords, live, factor_b, factor_c):
    n_i, n_j, n_k = sizes
    n_all = n_i * n_j * n_k
    slots, bi, bj, bk = blocks.shape
    rank = factor_b.shape[1]
    group_sizes = (n_j * n_k, n_i * n_k, n_i * n_j)
    spans = (GI_DEV * bi, factor_b.shape[0], factor_c.shape[0])
    extents = (bi, bj, bk)

    def message(mode):
        rows = extents[mode] // group_sizes[mode] + spans[mode] // extents[mode]
        return (group_sizes[mode], (rows + 7) // 8 * 8, rank)

    def buffer(*shape):
        return pltpu.VMEM(shape, F32)

    slices = [
        buffer(group_sizes[1], rank // group_sizes[1], rank),
        buffer(n_j, rank // group_sizes[1], rank),
        buffer(group_sizes[1], rank // group_sizes[1], rank),
    ]
    vmem = pl.BlockSpec(memory_space=pltpu.VMEM)
    far = pl.BlockSpec(memory_space=pltpu.HBM)
    shapes = [jax.ShapeDtypeStruct((span, rank), F32) for span in spans]
    return pl.pallas_call(
        functools.partial(kernel, sizes),
        out_shape=shapes,
        in_specs=[far, far, far, far],
        out_specs=[vmem] * 3,
        scratch_shapes=[
            pltpu.SMEM((coords.shape[0],), jnp.int32),
            pltpu.VMEM((bi * bj, bk), BF16),
            buffer(*factor_b.shape),
            buffer(*factor_c.shape),
            buffer(bi * bj, bk),
            pltpu.VMEM((bj, bi, bk), BF16),
            pltpu.VMEM((bk, bi * bj), BF16),
            buffer(max(bi, bj), rank),
            *slices,
            buffer(n_k, rank, rank),
            buffer(n_i, rank, rank),
            *slices,
            *[buffer(*message(mode)) for mode in (0, 2)],
            *[buffer(*message(mode)) for mode in (0, 2)],
            buffer(group_sizes[0], spans[0] // group_sizes[0], rank),
            buffer(group_sizes[1], bj + (spans[1] // bj + 7) // 8 * 8, rank),
            buffer(group_sizes[2], spans[2] // group_sizes[2], rank),
            buffer(3, 1, rank),
            buffer(n_all - group_sizes[0], 1, rank),
            buffer(n_j, 1, rank),
            buffer(n_all - group_sizes[2], 1, rank),
            pltpu.SemaphoreType.DMA((4,)),
            pltpu.SemaphoreType.DMA((2, 15)),
            pltpu.SemaphoreType.DMA((2, n_j)),
        ],
        compiler_params=pltpu.CompilerParams(
            collective_id=0, has_side_effects=True, vmem_limit_bytes=48 * 1024 * 1024
        ),
    )(
        *(
            pltpu.with_memory_space_constraint(array, pltpu.HBM)
            for array in (coords.reshape(coords.shape[0]), blocks.reshape(slots * bi * bj, bk), factor_b, factor_c)
        ),
    )


def solution(mesh):
    sizes = (mesh.shape["ia"], mesh.shape["ja"], mesh.shape["ka"])
    placed = (
        P(("ia", "ja", "ka"), None, None, None),
        P(None, ("ia", "ja", "ka")),
        P(("ia", "ja", "ka")),
        P("ja", None),
        P("ka", None),
    )
    return jax.shard_map(
        functools.partial(on_device, sizes),
        mesh=mesh,
        in_specs=placed,
        out_specs=(P("ia", None), P("ja", None), P("ka", None)),
        check_vma=False,
    )
```
